256 devices in a mesh: dp: 16 (over y, x_hi, core), tensor: 16 (over x_lo, z).
Axes of the slice: x: 4 (x_hi: 2, x_lo: 2; x = x_hi * 2 + x_lo), y: 4, z: 8, core: 2. Of those that a mesh axis runs over, the one named last changes fastest.
Arguments:
- gate_pre: bfloat16 [8192, 18432], P('dp', 'tensor'), may hold values from -6 to 6
- up_saved: bfloat16 [8192, 18432], P('dp', 'tensor'), may hold values from -6 to 6
- cotangent: bfloat16 [8192, 4608], P(('dp', 'tensor')), may hold values from -24 to 24
- down_weight: bfloat16 [4608, 18432], P('dp', 'tensor'), may hold values from -0.046875 to 0.046875
Outputs:
- grad_gate: bfloat16 [8192, 18432], P('dp', 'tensor')
- grad_up: bfloat16 [8192, 18432], P('dp', 'tensor')
- grad_down: bfloat16 [4608, 18432], P('dp', 'tensor')
The draws below stay inside these ranges and needn't reach their ends.
All inputs are finite; a program needn't handle non-finite values.
Results may differ from the reference program's by a relative error of at most 0.017.
Values may be sent and summed in bfloat16 or wider, within the bound.
A program may use at most 128 MiB of HBM per device.

```python
import jax
import jax.numpy as jnp
from jax import lax

D = 4608
FF = 18432
TOK = 512
TOKENS = 8192
N_DP = 16


def strengthened(entries, own_key, source, target, blocks, factor):
    owner, partner = [(jnp.arange(entries.shape[dim]) // (entries.shape[dim] // blocks)).reshape([-1 if axis == dim else 1 for axis in range(entries.ndim)]) for dim in (source, target)]
    chosen = jax.random.permutation(own_key, blocks)[partner]
    strong = (owner == chosen) | (owner == (partner + blocks // 2) % blocks)
    return jnp.where(strong, factor * entries, entries)


def level_of(own_key, dims, cuts, smallest, largest):
    level, own = 1.0, jax.random.fold_in(own_key, 6)
    for dim, shards_of in cuts:
        steps = jnp.exp(jax.random.uniform(jax.random.fold_in(own, dim), (shards_of,), jnp.float32, smallest / len(cuts), largest / len(cuts)))
        level = level * jnp.repeat(steps, dims[dim] // shards_of).reshape([-1 if axis == dim else 1 for axis in range(len(dims))])
    return level


def bell_draw(rng, shape, deviation, most, shards=(), kind=jnp.bfloat16):
    drawn = jax.random.normal(rng, shape, jnp.float32) * deviation
    if len(shards) > 0:
        drawn = level_of(rng, shape, shards, -0.22, 0.18) * drawn
    return jnp.clip(drawn, min=-most, max=most).astype(kind)


def bell_draw_with(rng, extent, spread, limit, split, heavy, held_as=jnp.bfloat16):
    result = spread * jax.random.normal(rng, extent, jnp.float32)
    if split:
        result = result * level_of(rng, extent, split, -0.22, 0.18)
    return jnp.clip(strengthened(result, jax.random.fold_in(rng, 3), *heavy), -limit, limit).astype(held_as)


def setup_inputs(seed: int = 0) -> dict:
    key_list = jax.random.split(jax.random.key(seed), 5)
    gate_pre = bell_draw(key_list[0], (TOKENS, FF), 1.0, 6.0, ((0, 16), (1, 16)))
    up_saved = bell_draw(key_list[1], (TOKENS, FF), 1.0, 6.0, ((0, 16), (1, 16)))
    cotangent = bell_draw_with(key_list[2], (TOKENS, D), 1.0, 24.0, ((0, 256),), (0, 1, 256, 6.0))
    down_weight = bell_draw(key_list[3], (D, FF), FF ** -0.5, 0.046875, ((0, 16), (1, 16)))
    return {"gate_pre": gate_pre, "up_saved": up_saved, "cotangent": cotangent, "down_weight": down_weight}


root_coef = 0.7978845608028654
cubic_coef = 0.044715


def gelu_parts(gate_f32):
    inner = root_coef * (gate_f32 + cubic_coef * gate_f32 * gate_f32 * gate_f32)
    tanh_val = jnp.tanh(inner)
    activated = 0.5 * gate_f32 * (1.0 + tanh_val)
    derivative = 0.5 * (1.0 + tanh_val) + 0.5 * gate_f32 * (1.0 - tanh_val * tanh_val) * root_coef * (1.0 + 3.0 * cubic_coef * gate_f32 * gate_f32)
    return activated, derivative


def reference(gate_pre, up_saved, cotangent, down_weight):
    gate_f32 = gate_pre.astype(jnp.float32)
    up_f32 = up_saved.astype(jnp.float32)
    activated, derivative = gelu_parts(gate_f32)
    hidden = (activated * up_f32).astype(jnp.bfloat16)
    grad_hidden = jnp.dot(cotangent, down_weight, preferred_element_type=jnp.float32)
    grad_gate = (grad_hidden * up_f32 * derivative).astype(jnp.bfloat16)
    grad_up = (grad_hidden * activated).astype(jnp.bfloat16)
    cot_groups = cotangent.reshape(N_DP, TOK, D)
    hid_groups = hidden.reshape(N_DP, TOK, FF)

    def accumulate(running, group_pair):
        cot_rows, hid_rows = group_pair
        partial_sum = lax.dot_general(cot_rows, hid_rows, (((0,), (0,)), ((), ())), preferred_element_type=jnp.float32)
        rounded = lax.optimization_barrier(partial_sum.astype(jnp.bfloat16))
        return running + rounded.astype(jnp.float32), None

    running, _ = lax.scan(accumulate, jnp.zeros((D, FF), jnp.float32), (cot_groups, hid_groups))
    return grad_gate, grad_up, running.astype(jnp.bfloat16)
```

```python
import functools

import jax
import jax.numpy as jnp
from jax import lax
from jax.experimental import pallas as pl
from jax.experimental.pallas import tpu as pltpu
from jax.sharding import PartitionSpec as P

MESH = pl.DeviceIdType.MESH
BF16, F32 = jnp.bfloat16, jnp.float32

root_coef = 0.7978845608028654
cubic_coef = 0.044715

D = 4608
FF = 1152
ROWS = 32
QD = 1152
OWN = 288
HALF = OWN // 2
TILE = 384
ORDER = (2, 1, 3, 0)
POS = {r: p for p, r in enumerate(ORDER)}
SUBS = (0, 1, 3, 2)
ROUNDS = ((0, 3), (3, 2), (5, 2), (7, 1))


def gelu_parts(gate_f32):
    inner = root_coef * (gate_f32 + cubic_coef * gate_f32 * gate_f32 * gate_f32)
    tanh_val = jnp.tanh(inner)
    activated = 0.5 * gate_f32 * (1.0 + tanh_val)
    derivative = 0.5 * (1.0 + tanh_val) + 0.5 * gate_f32 * (
        1.0 - tanh_val * tanh_val
    ) * root_coef * (1.0 + 3.0 * cubic_coef * gate_f32 * gate_f32)
    return (activated, derivative)


def kernel(
    gate, up, cot, weight, grad_gate, grad_up, grad_down,
    csrc, cbuf, wbuf, hbuf, act, uder, acc,
    peer_out, peer_in, kept, far_out, far_in, gd_out, gd_half, gd_in,
    c_s, c_r, z_s, z_r, w_s, w_r, h_s, h_r, p_s, p_r, f_s, f_r, g_s, g_r,
):
    dp, tensor = lax.axis_index("dp"), lax.axis_index("tensor")
    y, xh, c = dp // 4, (dp // 2) % 2, dp % 2
    xl, z = tensor // 8, tensor % 8
    x = xh * 2 + xl

    def at(dx=0, dy=0, dz=0, dc=0):
        nx, ny, nz, nc = (x + dx) % 4, (y + dy) % 4, (z + dz) % 8, (c + dc) % 2
        return (ny * 4 + (nx // 2) * 2 + nc, (nx % 2) * 8 + nz)

    started = []

    def send(src, dst, ss, rs, to):
        copy = pltpu.make_async_remote_copy(
            src_ref=src, dst_ref=dst, send_sem=ss, recv_sem=rs, device_id=to, device_id_type=MESH
        )
        copy.start()
        started.append(copy)
        return copy

    near = [(dx, dc) for dx in range(4) for dc in range(2) if (dx, dc) != (0, 0)]
    barrier = pltpu.get_barrier_semaphore()
    partners = [at(dx=dx, dc=dc) for dx, dc in near] + [at(dz=1), at(dz=7), at(dy=1), at(dy=3)]
    for partner in partners:
        pl.semaphore_signal(barrier, inc=1, device_id=partner, device_id_type=MESH)

    for p, r in enumerate(ORDER):
        start = pl.multiple_of(((y + r) % 4) * QD, 128)
        block = cot[:, pl.ds(start, QD)]
        for q in range(4):
            csrc[q, :, p * OWN : (p + 1) * OWN] = block[:, q * OWN : (q + 1) * OWN]
    wbuf[pl.ds(POS[0] * OWN, OWN), :] = weight[...]
    cbuf[0, c, x] = csrc[xh * 2 + c]

    pl.semaphore_wait(barrier, len(partners))

    c_copies = {}
    for i, (dx, dc) in enumerate(near):
        nq = (((x + dx) % 4) // 2) * 2 + (c + dc) % 2
        c_copies[dx, dc] = send(
            csrc.at[nq], cbuf.at[0, c, x], c_s.at[i], c_r.at[i], at(dx=dx, dc=dc)
        )

    def wrows(r, first=0, rows=OWN):
        return wbuf.at[pl.ds(POS[r] * OWN + first, rows)]

    w_up = send(wrows(0), wrows(3), w_s.at[0], w_r.at[0], at(dy=1))
    w_down = send(wrows(0), wrows(1), w_s.at[1], w_r.at[1], at(dy=3))

    def z_of(slot):
        return (z + (1 - 2 * (slot % 2)) * ((slot + 1) // 2) + 8) % 8

    def hidden(slot, _):
        zs = z_of(slot)
        up_f32 = up[:, zs].astype(F32)
        activated, derivative = gelu_parts(gate[:, zs].astype(F32))
        act[slot] = activated
        uder[slot] = up_f32 * derivative
        hbuf[slot, c, pl.ds(xh * 2, 2)] = (activated * up_f32).astype(BF16)
        return 0

    def ring(step, j):
        xs = (x + SUBS[j]) % 4
        out = []
        for way in range(2):
            if step == 3 and (j < 2) != (way == 0):
                out.append(None)
                continue
            src = 0 if step == 0 else 2 * step - 1 + way
            dst = 7 if step == 3 else 2 * step + 1 + way
            out.append(
                send(
                    cbuf.at[src, :, xs], cbuf.at[dst, :, xs],
                    z_s.at[way, step, j], z_r.at[way, step, j],
                    at(dz=1 if way == 0 else 7),
                )
            )
        return out

    ringed = {}

    def arrive(step, j):
        for copy in ringed[step, j]:
            if copy is not None:
                copy.wait_recv()

    def forward(step):
        for j in range(4):
            arrive(step - 1, j)
            ringed[step, j] = ring(step, j)

    h_copies = {}

    def send_h(i):
        mine = hbuf.at[pl.ds(2 * i, 2), c, pl.ds(xh * 2, 2)]
        h_copies["p", i] = send(mine, mine, h_s.at[0, i], h_r.at[0, i], at(dc=1))
        h_copies["x", i] = send(mine, mine, h_s.at[1, i], h_r.at[1, i], at(dx=2))

    def pass_h(i):
        h_copies["x", i].wait_recv()
        theirs = hbuf.at[pl.ds(2 * i, 2), c, pl.ds((1 - xh) * 2, 2)]
        h_copies["f", i] = send(theirs, theirs, h_s.at[2, i], h_r.at[2, i], at(dc=1))

    def arrive_h(i):
        h_copies["p", i].wait_recv()
        h_copies["f", i].wait_recv()

    for j in range(4):
        lax.fori_loop(2 * j, 2 * j + 2, hidden, 0)
        dx = (4 - SUBS[j]) % 4
        for dc in range(2):
            if (dx, dc) != (0, 0):
                c_copies[dx, dc].wait_recv()
        ringed[0, j] = ring(0, j)
    for i in range(4):
        send_h(i)

    forward(1)
    w_up.wait_recv()
    w_up2 = send(wrows(3, 0, HALF), wrows(2, 0, HALF), w_s.at[2], w_r.at[2], at(dy=1))
    w_down.wait_recv()
    w_down2 = send(
        wrows(1, HALF, HALF), wrows(2, HALF, HALF), w_s.at[3], w_r.at[3], at(dy=3)
    )
    pass_h(0)

    def grad_hidden(first, n, cp, store):
        @pl.loop(0, FF // TILE)
        def _(t):
            cols = pl.ds(pl.multiple_of(t * TILE, TILE), TILE)
            lhs = cbuf[pl.ds(first, n), cp].reshape(n * 128, QD)
            out = jnp.dot(lhs, wbuf[:, cols], preferred_element_type=F32)
            store(cols, out.reshape(n, 4, ROWS, TILE))

    p_copies, f_copies = {}, {}

    def partial_hidden(i):
        first, n = ROUNDS[i]
        slots = pl.ds(first, n)

        def to_peer(cols, out):
            peer_out[slots, :, :, cols] = out.astype(BF16)

        def keep(cols, out):
            kept[slots, :, :, cols] = out

        grad_hidden(first, n, 1 - c, to_peer)
        p_copies[i] = send(
            peer_out.at[slots], peer_in.at[slots], p_s.at[i], p_r.at[i], at(dc=1)
        )
        grad_hidden(first, n, c, keep)

    def add_peer(i):
        first, n = ROUNDS[i]
        p_copies[i].wait_recv()

        def one(slot, _):
            far = pl.ds((1 - xh) * 2, 2)
            total = kept[slot, far] + peer_in[slot, far].astype(F32)
            far_out[slot] = total.astype(BF16)
            return 0

        lax.fori_loop(first, first + n, one, 0)
        slots = pl.ds(first, n)
        f_copies[i] = send(
            far_out.at[slots], far_in.at[slots], f_s.at[i], f_r.at[i], at(dx=2)
        )

    def finish_hidden(i):
        first, n = ROUNDS[i]
        f_copies[i].wait_recv()

        def one(slot, _):
            zs = z_of(slot)
            near_x = pl.ds(xh * 2, 2)
            total = (
                kept[slot, near_x]
                + peer_in[slot, near_x].astype(F32)
                + far_in[slot].astype(F32)
            )
            grad_gate[:, zs] = (total * uder[slot]).astype(BF16)
            grad_up[:, zs] = (total * act[slot]).astype(BF16)
            return 0

        lax.fori_loop(first, first + n, one, 0)

    def partial_down(i, tile):
        first, n = ROUNDS[i]
        rows = pl.ds(pl.multiple_of(tile * TILE, TILE), TILE)
        lhs = cbuf[pl.ds(first, n), :, :, :, rows].reshape(n * 256, TILE)
        for t in range(FF // TILE):
            cols = slice(t * TILE, (t + 1) * TILE)
            rhs = hbuf[pl.ds(first, n), :, :, :, cols].reshape(n * 256, TILE)
            out = lax.dot_general(lhs, rhs, (((0,), (0,)), ((), ())), preferred_element_type=F32)
            if i == 0:
                acc[rows, cols] = out
            else:
                acc[rows, cols] += out

    def down_round(i):
        @pl.loop(0, QD // TILE)
        def _(tile):
            partial_down(i, tile)

    ringed[2, 0] = None
    for j in range(2):
        arrive(1, j)
        ringed[2, j] = ring(2, j)
    pass_h(1)
    arrive_h(0)
    arrive_h(1)
    down_round(0)
    for j in range(2, 4):
        arrive(1, j)
        ringed[2, j] = ring(2, j)
    w_up2.wait_recv()
    w_down2.wait_recv()
    partial_hidden(0)
    add_peer(0)
    pass_h(2)
    partial_hidden(1)
    add_peer(1)
    for j in range(2):
        arrive(2, j)
        ringed[3, j] = ring(3, j)
    arrive_h(2)
    down_round(1)
    pass_h(3)
    for j in range(2, 4):
        arrive(2, j)
        ringed[3, j] = ring(3, j)
    partial_hidden(2)
    add_peer(2)
    arrive_h(3)
    down_round(2)
    for j in range(4):
        arrive(3, j)

    def gd_rows(r, first=0, rows=OWN):
        return pl.ds(POS[r] * OWN + first, rows)

    def round_gd(r):
        gd_out[gd_rows(r)] = acc[gd_rows(r), :].astype(BF16)

    g = {}

    def send_gd(name, k, rows, dst, to):
        g[name] = send(gd_out.at[rows], dst, g_s.at[k], g_r.at[k], to)

    upward, downward = at(dy=1), at(dy=3)
    partial_down(3, 0)
    round_gd(2)
    send_gd("u2", 0, gd_rows(2, 0, HALF), gd_half.at[0], upward)
    send_gd("d2", 1, gd_rows(2, HALF, HALF), gd_half.at[1], downward)
    partial_down(3, 1)
    round_gd(1)
    send_gd("u1", 2, gd_rows(1, HALF, HALF), gd_in.at[0, pl.ds(HALF, HALF)], upward)
    partial_down(3, 2)
    round_gd(3)
    send_gd("d1", 3, gd_rows(3, 0, HALF), gd_in.at[1, pl.ds(0, HALF)], downward)
    partial_hidden(3)
    add_peer(3)
    finish_hidden(0)
    g["u2"].wait_recv()
    rows = gd_rows(1, 0, HALF)
    gd_out[rows] = (acc[rows, :] + gd_half[0].astype(F32)).astype(BF16)
    send_gd("u3", 4, rows, gd_in.at[0, pl.ds(0, HALF)], upward)
    g["d2"].wait_recv()
    rows = gd_rows(3, HALF, HALF)
    gd_out[rows] = (acc[rows, :] + gd_half[1].astype(F32)).astype(BF16)
    send_gd("d3", 5, rows, gd_in.at[1, pl.ds(HALF, HALF)], downward)
    finish_hidden(1)
    finish_hidden(2)
    finish_hidden(3)
    g["u1"].wait_recv()
    g["d1"].wait_recv()
    g["u3"].wait_recv()
    g["d3"].wait_recv()
    grad_down[...] = (
        acc[gd_rows(0), :] + gd_in[0].astype(F32) + gd_in[1].astype(F32)
    ).astype(BF16)
    for copy in started:
        copy.wait_send()


def on_device(gate_pre, up_saved, cotangent, down_weight):
    vmem = pl.BlockSpec(memory_space=pltpu.VMEM)
    dma = pltpu.SemaphoreType.DMA
    tokens = (2, 8, ROWS, FF)
    grad_gate, grad_up, grad_down = pl.pallas_call(
        kernel,
        name="ffn_down_backward",
        out_shape=(
            jax.ShapeDtypeStruct(tokens, BF16),
            jax.ShapeDtypeStruct(tokens, BF16),
            jax.ShapeDtypeStruct((OWN, FF), BF16),
        ),
        in_specs=[vmem] * 4,
        out_specs=(vmem,) * 3,
        scratch_shapes=[
            pltpu.VMEM((4, ROWS, QD), BF16),
            pltpu.VMEM((8, 2, 4, ROWS, QD), BF16),
            pltpu.VMEM((QD, FF), BF16),
            pltpu.VMEM((8, 2, 4, ROWS, FF), BF16),
            pltpu.VMEM((8, 2, ROWS, FF), F32),
            pltpu.VMEM((8, 2, ROWS, FF), F32),
            pltpu.VMEM((QD, FF), F32),
            pltpu.VMEM((8, 4, ROWS, FF), BF16),
            pltpu.VMEM((8, 4, ROWS, FF), BF16),
            pltpu.VMEM((8, 4, ROWS, FF), F32),
            pltpu.VMEM((8, 2, ROWS, FF), BF16),
            pltpu.VMEM((8, 2, ROWS, FF), BF16),
            pltpu.VMEM((QD, FF), BF16),
            pltpu.VMEM((2, HALF, FF), BF16),
            pltpu.VMEM((2, OWN, FF), BF16),
            dma((7,)), dma((7,)),
            dma((2, 4, 4)), dma((2, 4, 4)),
            dma((4,)), dma((4,)),
            dma((3, 4)), dma((3, 4)),
            dma((4,)), dma((4,)),
            dma((4,)), dma((4,)),
            dma((6,)), dma((6,)),
        ],
        compiler_params=pltpu.CompilerParams(
            collective_id=0, has_side_effects=True, vmem_limit_bytes=60 << 20
        ),
        cost_estimate=pl.CostEstimate(
            flops=4 * 2048 * QD * FF, bytes_accessed=7 << 20, transcendentals=512 * FF
        ),
    )(
        gate_pre.reshape(tokens), up_saved.reshape(tokens), cotangent, down_weight
    )
    return (grad_gate.reshape(512, FF), grad_up.reshape(512, FF), grad_down)


def solution(mesh):
    in_specs = (P("dp", "tensor"), P("dp", "tensor"), P(("dp", "tensor"), None), P("dp", "tensor"))
    out_specs = (P("dp", "tensor"), P("dp", "tensor"), P("dp", "tensor"))
    return jax.shard_map(
        on_device, mesh=mesh, in_specs=in_specs, out_specs=out_specs, check_vma=False
    )
```

```python
import functools

import jax
import jax.numpy as jnp
from jax import lax
from jax.experimental import pallas as pl
from jax.experimental.pallas import tpu as pltpu
from jax.sharding import PartitionSpec as P

MESH = pl.DeviceIdType.MESH
BF16, F32 = jnp.bfloat16, jnp.float32

root_coef = 0.7978845608028654
cubic_coef = 0.044715

D = 4608
FF = 1152
ROWS = 32
QD = 1152
OWN = 288
HALF = OWN // 2
TILE = 384
ORDER = (2, 1, 3, 0)
POS = {r: p for p, r in enumerate(ORDER)}
SUBS = (0, 1, 3, 2)
ROUNDS = ((0, 3), (3, 2), (5, 3))
CHUNKS = ((0, 384), (384, 256), (640, 256), (896, 256))


def gelu_parts(gate_f32):
    inner = root_coef * (gate_f32 + cubic_coef * gate_f32 * gate_f32 * gate_f32)
    tanh_val = jnp.tanh(inner)
    activated = 0.5 * gate_f32 * (1.0 + tanh_val)
    derivative = 0.5 * (1.0 + tanh_val) + 0.5 * gate_f32 * (
        1.0 - tanh_val * tanh_val
    ) * root_coef * (1.0 + 3.0 * cubic_coef * gate_f32 * gate_f32)
    return (activated, derivative)


def kernel(
    gate_hbm, up_hbm, cot_hbm, weight, grad_gate, grad_up, grad_down,
    gate, up, cot, csrc, cbuf, wbuf, hbuf, act, uder, acc,
    peer_out, peer_in, kept, far_out, far_in, gd_out, gd_half, gd_in,
    in_s, c_s, c_r, z_s, z_r, w_s, w_r, h_s, h_r, p_s, p_r, f_s, f_r, g_s, g_r,
):
    dp, tensor = lax.axis_index("dp"), lax.axis_index("tensor")
    y, xh, c = dp // 4, (dp // 2) % 2, dp % 2
    xl, z = tensor // 8, tensor % 8
    x = xh * 2 + xl

    def at(dx=0, dy=0, dz=0, dc=0):
        nx, ny, nz, nc = (x + dx) % 4, (y + dy) % 4, (z + dz) % 8, (c + dc) % 2
        return (ny * 4 + (nx // 2) * 2 + nc, (nx % 2) * 8 + nz)

    started = []

    def send(src, dst, ss, rs, to):
        copy = pltpu.make_async_remote_copy(
            src_ref=src, dst_ref=dst, send_sem=ss, recv_sem=rs, device_id=to, device_id_type=MESH
        )
        copy.start()
        started.append(copy)
        return copy

    near = [(dx, dc) for dx in range(4) for dc in range(2) if (dx, dc) != (0, 0)]
    barrier = pltpu.get_barrier_semaphore()
    partners = [at(dx=dx, dc=dc) for dx, dc in near] + [at(dz=1), at(dz=7), at(dy=1), at(dy=3)]
    for partner in partners:
        pl.semaphore_signal(barrier, inc=1, device_id=partner, device_id_type=MESH)

    def fetch(k, src, dst):
        copy = pltpu.make_async_copy(src, dst, in_s.at[k])
        copy.start()
        return copy

    cot_copy = fetch(0, cot_hbm, cot)
    weight_copy = fetch(1, weight, wbuf.at[pl.ds(POS[0] * OWN, OWN)])
    gate_copy = fetch(2, gate_hbm, gate)
    up_copy = fetch(3, up_hbm, up)
    cot_copy.wait()
    for p, r in enumerate(ORDER):
        start = pl.multiple_of(((y + r) % 4) * QD, 128)
        block = cot[:, pl.ds(start, QD)]
        for q in range(4):
            csrc[q, :, p * OWN : (p + 1) * OWN] = block[:, q * OWN : (q + 1) * OWN]
    cbuf[0, c, x] = csrc[xh * 2 + c]

    pl.semaphore_wait(barrier, len(partners))

    c_copies = {}

    def send_c(*dxs):
        for i, (dx, dc) in enumerate(near):
            if dx in dxs:
                nq = (((x + dx) % 4) // 2) * 2 + (c + dc) % 2
                c_copies[dx, dc] = send(
                    csrc.at[nq], cbuf.at[0, c, x], c_s.at[i], c_r.at[i], at(dx=dx, dc=dc)
                )

    send_c(0, 1, 3)

    def wrows(r, first=0, rows=OWN):
        return wbuf.at[pl.ds(POS[r] * OWN + first, rows)]

    weight_copy.wait()
    w_up = send(wrows(0), wrows(3), w_s.at[0], w_r.at[0], at(dy=1))
    w_down = send(wrows(0), wrows(1), w_s.at[1], w_r.at[1], at(dy=3))

    def z_of(slot):
        return (z + (1 - 2 * (slot % 2)) * ((slot + 1) // 2) + 8) % 8

    def hidden(slot, _):
        zs = z_of(slot)
        up_f32 = up[:, zs].astype(F32)
        activated, derivative = gelu_parts(gate[:, zs].astype(F32))
        act[slot] = activated
        uder[slot] = up_f32 * derivative
        hbuf[slot, c, pl.ds(xh * 2, 2)] = (activated * up_f32).astype(BF16)
        return 0

    def send_z(way, k, src, dst):
        to = at(dz=1 if way == 0 else 7)
        return send(src, dst, z_s.at[way, k], z_r.at[way, k], to)

    def ring(step, j):
        xs = (x + SUBS[j]) % 4
        out = []
        for way in range(2):
            src = 0 if step == 0 else 2 * step - 1 + way
            src, dst = cbuf.at[src, :, xs], cbuf.at[2 * step + 1 + way, :, xs]
            out.append(send_z(way, 4 * step + j, src, dst))
        return out

    def ring_first(j):
        xs, cols = (x + SUBS[j]) % 4, pl.ds(*CHUNKS[0])
        return [
            send_z(
                way, 8 + j,
                cbuf.at[3 + way, :, xs, :, cols], cbuf.at[5 + way, :, xs, :, cols],
            )
            for way in range(2)
        ]

    def ring_chunk(k):
        cols = pl.ds(*CHUNKS[k])
        return [
            send_z(
                way, 11 + k,
                cbuf.at[3 + way, :, :, :, cols], cbuf.at[5 + way, :, :, :, cols],
            )
            for way in range(2)
        ]

    def ring_last(k, j=None):
        cols = pl.ds(*CHUNKS[k])
        xs = pl.ds(0, 4) if j is None else (x + SUBS[j]) % 4
        sem = 14 + k if j is None else 18 + j
        return [
            send_z(
                way, sem, cbuf.at[5 + way, way, xs, :, cols], cbuf.at[7, way, xs, :, cols]
            )
            for way in range(2)
        ]

    ringed = {}

    def arrive(*name):
        for copy in ringed[name]:
            copy.wait_recv()

    def forward(step):
        for j in range(4):
            arrive(step - 1, j)
            ringed[step, j] = ring(step, j)

    h_copies = {}

    def send_h(i):
        mine = hbuf.at[pl.ds(2 * i, 2), c, pl.ds(xh * 2, 2)]
        h_copies["p", i] = send(mine, mine, h_s.at[0, i], h_r.at[0, i], at(dc=1))
        h_copies["x", i] = send(mine, mine, h_s.at[1, i], h_r.at[1, i], at(dx=2))

    def pass_h(i):
        h_copies["x", i].wait_recv()
        theirs = hbuf.at[pl.ds(2 * i, 2), c, pl.ds((1 - xh) * 2, 2)]
        h_copies["f", i] = send(theirs, theirs, h_s.at[2, i], h_r.at[2, i], at(dc=1))

    def arrive_h(i):
        h_copies["p", i].wait_recv()
        h_copies["f", i].wait_recv()

    gate_copy.wait()
    up_copy.wait()
    for j in range(4):
        lax.fori_loop(2 * j, 2 * j + 2, hidden, 0)
        dx = (4 - SUBS[j]) % 4
        for dc in range(2):
            if (dx, dc) != (0, 0):
                c_copies[dx, dc].wait_recv()
        ringed[0, j] = ring(0, j)
        if j == 2:
            send_c(2)
    for i in range(4):
        send_h(i)

    forward(1)
    w_up.wait_recv()
    w_up2 = send(wrows(3, 0, HALF), wrows(2, 0, HALF), w_s.at[2], w_r.at[2], at(dy=1))
    w_down.wait_recv()
    w_down2 = send(
        wrows(1, HALF, HALF), wrows(2, HALF, HALF), w_s.at[3], w_r.at[3], at(dy=3)
    )
    pass_h(0)

    def grad_hidden(first, n, cp, store):
        @pl.loop(0, FF // TILE)
        def _(t):
            cols = pl.ds(pl.multiple_of(t * TILE, TILE), TILE)
            lhs = cbuf[pl.ds(first, n), cp].reshape(n * 128, QD)
            out = jnp.dot(lhs, wbuf[:, cols], preferred_element_type=F32)
            store(cols, out.reshape(n, 4, ROWS, TILE))

    p_copies, f_copies = {}, {}

    def partial_hidden(i):
        first, n = ROUNDS[i]
        slots = pl.ds(first, n)

        def to_peer(cols, out):
            peer_out[slots, :, :, cols] = out.astype(BF16)

        def keep(cols, out):
            kept[slots, :, :, cols] = out

        grad_hidden(first, n, 1 - c, to_peer)
        p_copies[i] = send(
            peer_out.at[slots], peer_in.at[slots], p_s.at[i], p_r.at[i], at(dc=1)
        )
        grad_hidden(first, n, c, keep)

    def add_peer(i):
        first, n = ROUNDS[i]
        p_copies[i].wait_recv()

        def one(slot, _):
            far = pl.ds((1 - xh) * 2, 2)
            total = kept[slot, far] + peer_in[slot, far].astype(F32)
            far_out[slot] = total.astype(BF16)
            return 0

        lax.fori_loop(first, first + n, one, 0)
        slots = pl.ds(first, n)
        f_copies[i] = send(
            far_out.at[slots], far_in.at[slots], f_s.at[i], f_r.at[i], at(dx=2)
        )

    def finish_hidden(i):
        first, n = ROUNDS[i]
        f_copies[i].wait_recv()

        def one(slot, _):
            zs = z_of(slot)
            near_x = pl.ds(xh * 2, 2)
            total = (
                kept[slot, near_x]
                + peer_in[slot, near_x].astype(F32)
                + far_in[slot].astype(F32)
            )
            grad_gate[:, zs] = (total * uder[slot]).astype(BF16)
            grad_up[:, zs] = (total * act[slot]).astype(BF16)
            return 0

        lax.fori_loop(first, first + n, one, 0)

    def partial_down(i, start, size):
        first, n = ROUNDS[i]
        rows = pl.ds(start, size)
        lhs = cbuf[pl.ds(first, n), :, :, :, rows].reshape(n * 256, size)
        for t in range(FF // TILE):
            cols = slice(t * TILE, (t + 1) * TILE)
            rhs = hbuf[pl.ds(first, n), :, :, :, cols].reshape(n * 256, TILE)
            out = lax.dot_general(lhs, rhs, (((0,), (0,)), ((), ())), preferred_element_type=F32)
            if i == 0:
                acc[rows, cols] = out
            else:
                acc[rows, cols] += out

    def down_round(i):
        @pl.loop(0, QD // TILE)
        def _(tile):
            partial_down(i, pl.multiple_of(tile * TILE, TILE), TILE)

    for j in range(2):
        arrive(1, j)
        ringed["first", j] = ring_first(j)
    pass_h(1)
    arrive_h(0)
    arrive_h(1)
    down_round(0)
    for j in range(2, 4):
        arrive(1, j)
        ringed["first", j] = ring_first(j)
    w_up2.wait_recv()
    w_down2.wait_recv()
    partial_hidden(0)
    pass_h(2)
    for j in range(4):
        arrive("first", j)
        ringed["last", 0, j] = ring_last(0, j)
    ringed["chunk", 1] = ring_chunk(1)
    ringed["chunk", 2] = ring_chunk(2)
    partial_hidden(1)
    arrive_h(2)
    pass_h(3)
    add_peer(0)
    add_peer(1)
    arrive("chunk", 1)
    ringed["last", 1] = ring_last(1)
    ringed["chunk", 3] = ring_chunk(3)
    down_round(1)
    arrive_h(3)

    def gd_rows(r, first=0, rows=OWN):
        return pl.ds(POS[r] * OWN + first, rows)

    def round_gd(r):
        gd_out[gd_rows(r)] = acc[gd_rows(r), :].astype(BF16)

    g = {}

    def send_gd(name, k, rows, dst, to):
        g[name] = send(gd_out.at[rows], dst, g_s.at[k], g_r.at[k], to)

    upward, downward = at(dy=1), at(dy=3)
    for j in range(4):
        arrive("last", 0, j)
    partial_down(2, *CHUNKS[0])
    round_gd(2)
    send_gd("u2", 0, gd_rows(2, 0, HALF), gd_half.at[0], upward)
    send_gd("d2", 1, gd_rows(2, HALF, HALF), gd_half.at[1], downward)
    arrive("chunk", 2)
    ringed["last", 2] = ring_last(2)
    arrive("last", 1)
    partial_down(2, *CHUNKS[1])
    round_gd(1)
    send_gd("u1", 2, gd_rows(1, HALF, HALF), gd_in.at[0, pl.ds(HALF, HALF)], upward)
    arrive("chunk", 3)
    ringed["last", 3] = ring_last(3)
    arrive("last", 2)
    partial_down(2, *CHUNKS[2])
    round_gd(3)
    send_gd("d1", 3, gd_rows(3, 0, HALF), gd_in.at[1, pl.ds(0, HALF)], downward)
    g["u2"].wait_recv()
    rows = gd_rows(1, 0, HALF)
    gd_out[rows] = (acc[rows, :] + gd_half[0].astype(F32)).astype(BF16)
    send_gd("u3", 4, rows, gd_in.at[0, pl.ds(0, HALF)], upward)
    arrive("last", 3)
    partial_hidden(2)
    add_peer(2)
    g["d2"].wait_recv()
    rows = gd_rows(3, HALF, HALF)
    gd_out[rows] = (acc[rows, :] + gd_half[1].astype(F32)).astype(BF16)
    send_gd("d3", 5, rows, gd_in.at[1, pl.ds(HALF, HALF)], downward)
    partial_down(2, *CHUNKS[3])
    finish_hidden(0)
    finish_hidden(1)
    finish_hidden(2)
    g["u1"].wait_recv()
    g["d1"].wait_recv()
    g["u3"].wait_recv()
    g["d3"].wait_recv()
    grad_down[...] = (
        acc[gd_rows(0), :] + gd_in[0].astype(F32) + gd_in[1].astype(F32)
    ).astype(BF16)
    for copy in started:
        copy.wait_send()


def write_out(*refs):
    copies = [
        pltpu.make_async_copy(refs[i], refs[3 + i], refs[6].at[i]) for i in range(3)
    ]
    for copy in copies:
        copy.start()
    for copy in copies:
        copy.wait()


def on_device(gate_pre, up_saved, cotangent, down_weight):
    vmem = pl.BlockSpec(memory_space=pltpu.VMEM)
    dma = pltpu.SemaphoreType.DMA
    tokens = (2, 8, ROWS, FF)
    shapes = (tokens, tokens, (OWN, FF))
    results = pl.pallas_call(
        kernel,
        name="ffn_down_backward",
        out_shape=tuple(pltpu.VMEM(shape, BF16) for shape in shapes),
        in_specs=[pl.BlockSpec(memory_space=pl.ANY)] * 4,
        out_specs=(vmem,) * 3,
        scratch_shapes=[
            pltpu.VMEM(tokens, BF16),
            pltpu.VMEM(tokens, BF16),
            pltpu.VMEM((ROWS, D), BF16),
            pltpu.VMEM((4, ROWS, QD), BF16),
            pltpu.VMEM((8, 2, 4, ROWS, QD), BF16),
            pltpu.VMEM((QD, FF), BF16),
            pltpu.VMEM((8, 2, 4, ROWS, FF), BF16),
            pltpu.VMEM((8, 2, ROWS, FF), F32),
            pltpu.VMEM((8, 2, ROWS, FF), F32),
            pltpu.VMEM((QD, FF), F32),
            pltpu.VMEM((8, 4, ROWS, FF), BF16),
            pltpu.VMEM((8, 4, ROWS, FF), BF16),
            pltpu.VMEM((8, 4, ROWS, FF), F32),
            pltpu.VMEM((8, 2, ROWS, FF), BF16),
            pltpu.VMEM((8, 2, ROWS, FF), BF16),
            pltpu.VMEM((QD, FF), BF16),
            pltpu.VMEM((2, HALF, FF), BF16),
            pltpu.VMEM((2, OWN, FF), BF16),
            dma((4,)), dma((7,)), dma((7,)),
            dma((2, 22)), dma((2, 22)),
            dma((4,)), dma((4,)),
            dma((3, 4)), dma((3, 4)),
            dma((3,)), dma((3,)),
            dma((3,)), dma((3,)),
            dma((6,)), dma((6,)),
        ],
        compiler_params=pltpu.CompilerParams(
            collective_id=0, has_side_effects=True, vmem_limit_bytes=52 << 20
        ),
        cost_estimate=pl.CostEstimate(
            flops=4 * 2048 * QD * FF, bytes_accessed=7 << 20, transcendentals=512 * FF
        ),
    )(
        gate_pre.reshape(tokens), up_saved.reshape(tokens), cotangent, down_weight
    )
    grad_gate, grad_up, grad_down = pl.pallas_call(
        write_out,
        name="write_out",
        out_shape=tuple(jax.ShapeDtypeStruct(shape, BF16) for shape in shapes),
        in_specs=[vmem] * 3,
        out_specs=(pl.BlockSpec(memory_space=pl.ANY),) * 3,
        scratch_shapes=[dma((3,))],
        compiler_params=pltpu.CompilerParams(vmem_limit_bytes=8 << 20),
    )(*[pltpu.with_memory_space_constraint(r, pltpu.VMEM) for r in results])
    return (grad_gate.reshape(512, FF), grad_up.reshape(512, FF), grad_down)


def solution(mesh):
    in_specs = (P("dp", "tensor"), P("dp", "tensor"), P(("dp", "tensor"), None), P("dp", "tensor"))
    out_specs = (P("dp", "tensor"), P("dp", "tensor"), P("dp", "tensor"))
    return jax.shard_map(
        on_device, mesh=mesh, in_specs=in_specs, out_specs=out_specs, check_vma=False
    )
```

```python
import functools

import jax
import jax.numpy as jnp
from jax import lax
from jax.experimental import pallas as pl
from jax.experimental.pallas import tpu as pltpu
from jax.sharding import PartitionSpec as P

MESH = pl.DeviceIdType.MESH
BF16, F32 = jnp.bfloat16, jnp.float32

root_coef = 0.7978845608028654
cubic_coef = 0.044715

D = 4608
FF = 1152
ROWS = 32
QD = 1152
OWN = 288
HALF = OWN // 2
TILE = 384
UNITS = ((2, 0), (2, 1), (1, 1), (3, 0), (1, 0), (3, 1), (0, 0), (0, 1))
POS = {unit: k * HALF for k, unit in enumerate(UNITS)}
SUBS = (0, 1, 3, 2)
ROUNDS = ((0, 3), (3, 2), (5, 2), (7, 1))
FAR = ((0, 1), (1, 2), (3, 2), (5, 2), (7, 1))
DOWN = ((0, 3), (3, 2), (5, 3))
CHUNKS = ((0, 384), (384, 256), (640, 256), (896, 256))


def gelu_parts(gate_f32):
    inner = root_coef * (gate_f32 + cubic_coef * gate_f32 * gate_f32 * gate_f32)
    tanh_val = jnp.tanh(inner)
    activated = 0.5 * gate_f32 * (1.0 + tanh_val)
    derivative = 0.5 * (1.0 + tanh_val) + 0.5 * gate_f32 * (
        1.0 - tanh_val * tanh_val
    ) * root_coef * (1.0 + 3.0 * cubic_coef * gate_f32 * gate_f32)
    return (activated, derivative)


def kernel(
    gate_hbm, up_hbm, cot_hbm, weight, grad_gate, grad_up, grad_down,
    gate, up, cot, csrc, cbuf, wbuf, hbuf, act, uder, acc,
    peer_out, peer_in, kept, theirs_acc, far_out, far_in, gd_out, gd_half, gd_in,
    in_s, c_s, c_r, z_s, z_r, w_s, w_r, h_s, h_r, p_s, p_r, f_s, f_r, g_s, g_r,
):
    dp, tensor = lax.axis_index("dp"), lax.axis_index("tensor")
    y, xh, c = dp // 4, (dp // 2) % 2, dp % 2
    xl, z = tensor // 8, tensor % 8
    x = xh * 2 + xl

    def at(dx=0, dy=0, dz=0, dc=0):
        nx, ny, nz, nc = (x + dx) % 4, (y + dy) % 4, (z + dz) % 8, (c + dc) % 2
        return (ny * 4 + (nx // 2) * 2 + nc, (nx % 2) * 8 + nz)

    started = []

    def send(src, dst, ss, rs, to):
        copy = pltpu.make_async_remote_copy(
            src_ref=src, dst_ref=dst, send_sem=ss, recv_sem=rs, device_id=to, device_id_type=MESH
        )
        copy.start()
        started.append(copy)
        return copy

    near = [(dx, dc) for dx in range(4) for dc in range(2) if (dx, dc) != (0, 0)]
    barrier = pltpu.get_barrier_semaphore()
    partners = [at(dx=dx, dc=dc) for dx, dc in near] + [at(dz=1), at(dz=7), at(dy=1), at(dy=3)]
    for partner in partners:
        pl.semaphore_signal(barrier, inc=1, device_id=partner, device_id_type=MESH)

    def fetch(k, src, dst):
        copy = pltpu.make_async_copy(src, dst, in_s.at[k])
        copy.start()
        return copy

    cot_copy = fetch(0, cot_hbm, cot)
    weight_copy = fetch(1, weight, wbuf.at[pl.ds(POS[0, 0], OWN)])
    gate_copy = fetch(2, gate_hbm, gate)
    up_copy = fetch(3, up_hbm, up)
    cot_copy.wait()
    for (r, half), pos in POS.items():
        start = pl.multiple_of(((y + r) % 4) * QD, 128)
        block = cot[:, pl.ds(start, QD)]
        for q in range(4):
            first = q * OWN + half * HALF
            csrc[q, :, pos : pos + HALF] = block[:, first : first + HALF]
    cbuf[0, c, x] = csrc[xh * 2 + c]

    pl.semaphore_wait(barrier, len(partners))

    c_copies = {}

    def send_c(*dxs):
        for i, (dx, dc) in enumerate(near):
            if dx in dxs:
                nq = (((x + dx) % 4) // 2) * 2 + (c + dc) % 2
                c_copies[dx, dc] = send(
                    csrc.at[nq], cbuf.at[0, c, x], c_s.at[i], c_r.at[i], at(dx=dx, dc=dc)
                )

    send_c(0, 1, 3)

    def rows(r, half):
        return pl.ds(POS[r, half], HALF)

    def send_w(k, src, dst, to):
        return send(wbuf.at[rows(*src)], wbuf.at[rows(*dst)], w_s.at[k], w_r.at[k], to)

    upward, downward = at(dy=1), at(dy=3)
    weight_copy.wait()
    w_up = send_w(0, (0, 0), (3, 0), upward)
    w_down = send_w(1, (0, 1), (1, 1), downward)
    w_rest = [send_w(2, (0, 1), (3, 1), upward), send_w(3, (0, 0), (1, 0), downward)]

    def z_of(slot):
        return (z + (1 - 2 * (slot % 2)) * ((slot + 1) // 2) + 8) % 8

    def hidden(slot, _):
        zs = z_of(slot)
        up_f32 = up[:, zs].astype(F32)
        activated, derivative = gelu_parts(gate[:, zs].astype(F32))
        act[slot] = activated
        uder[slot] = up_f32 * derivative
        hbuf[slot, c, pl.ds(xh * 2, 2)] = (activated * up_f32).astype(BF16)
        return 0

    def send_z(way, k, src, dst):
        to = at(dz=1 if way == 0 else 7)
        return send(src, dst, z_s.at[way, k], z_r.at[way, k], to)

    def ring(step, j):
        xs = (x + SUBS[j]) % 4
        out = []
        for way in range(2):
            src = 0 if step == 0 else 2 * step - 1 + way
            src, dst = cbuf.at[src, :, xs], cbuf.at[2 * step + 1 + way, :, xs]
            out.append(send_z(way, 4 * step + j, src, dst))
        return out

    def ring_first(j):
        xs, cols = (x + SUBS[j]) % 4, pl.ds(*CHUNKS[0])
        return [
            send_z(
                way, 8 + j,
                cbuf.at[3 + way, :, xs, :, cols], cbuf.at[5 + way, :, xs, :, cols],
            )
            for way in range(2)
        ]

    def ring_chunk(k):
        cols = pl.ds(*CHUNKS[k])
        return [
            send_z(
                way, 11 + k,
                cbuf.at[3 + way, :, :, :, cols], cbuf.at[5 + way, :, :, :, cols],
            )
            for way in range(2)
        ]

    def ring_last(k, j=None):
        cols = pl.ds(*CHUNKS[k])
        xs = pl.ds(0, 4) if j is None else (x + SUBS[j]) % 4
        sem = 14 + k if j is None else 18 + j
        return [
            send_z(
                way, sem, cbuf.at[5 + way, way, xs, :, cols], cbuf.at[7, way, xs, :, cols]
            )
            for way in range(2)
        ]

    ringed = {}

    def arrive(*name):
        for copy in ringed[name]:
            copy.wait_recv()

    def forward(step):
        for j in range(4):
            arrive(step - 1, j)
            ringed[step, j] = ring(step, j)

    h_copies = {}

    def send_h(i):
        mine = hbuf.at[pl.ds(2 * i, 2), c, pl.ds(xh * 2, 2)]
        h_copies["p", i] = send(mine, mine, h_s.at[0, i], h_r.at[0, i], at(dc=1))
        h_copies["x", i] = send(mine, mine, h_s.at[1, i], h_r.at[1, i], at(dx=2))

    def pass_h(i):
        h_copies["x", i].wait_recv()
        theirs = hbuf.at[pl.ds(2 * i, 2), c, pl.ds((1 - xh) * 2, 2)]
        h_copies["f", i] = send(theirs, theirs, h_s.at[2, i], h_r.at[2, i], at(dc=1))

    def arrive_h(i):
        h_copies["p", i].wait_recv()
        h_copies["f", i].wait_recv()

    gate_copy.wait()
    up_copy.wait()
    lax.fori_loop(0, 8, hidden, 0)
    for j in range(4):
        dx = (4 - SUBS[j]) % 4
        for dc in range(2):
            if (dx, dc) != (0, 0):
                c_copies[dx, dc].wait_recv()
        ringed[0, j] = ring(0, j)
        if j == 2:
            send_c(2)
            for i in range(4):
                send_h(i)

    forward(1)
    w_up.wait_recv()
    w_rest.append(send_w(4, (3, 0), (2, 0), upward))
    w_down.wait_recv()
    w_rest.append(send_w(5, (1, 1), (2, 1), downward))
    pass_h(0)

    p_copies, f_copies = {}, {}

    def partial_hidden(i, start=0, size=QD):
        first, n = ROUNDS[i]
        begin, end = start == 0, start + size == QD
        cols = pl.ds(start, size)

        def one(slot, _):
            lhs = jnp.concatenate(
                [cbuf[slot, cp, :, :, cols].reshape(128, size) for cp in (1 - c, c)]
            )
            out = jnp.dot(lhs, wbuf[cols, :], preferred_element_type=F32)
            theirs, mine = out.reshape(2, 4, ROWS, FF)
            if not begin:
                theirs += theirs_acc[slot - 5]
                mine += kept[slot]
            kept[slot] = mine
            if end:
                peer_out[slot] = theirs.astype(BF16)
            else:
                theirs_acc[slot - 5] = theirs
            return 0

        lax.fori_loop(first, first + n, one, 0)
        if end:
            slots = pl.ds(first, n)
            p_copies[i] = send(
                peer_out.at[slots], peer_in.at[slots], p_s.at[i], p_r.at[i], at(dc=1)
            )

    def add_peer(i):
        first, n = ROUNDS[i]
        p_copies[i].wait_recv()

        def one(slot, _):
            far = pl.ds((1 - xh) * 2, 2)
            total = kept[slot, far] + peer_in[slot, far].astype(F32)
            far_out[slot] = total.astype(BF16)
            return 0

        lax.fori_loop(first, first + n, one, 0)

    def send_far(i):
        slots = pl.ds(*FAR[i])
        f_copies[i] = send(
            far_out.at[slots], far_in.at[slots], f_s.at[i], f_r.at[i], at(dx=2)
        )

    def finish_hidden(i):
        first, n = FAR[i]
        f_copies[i].wait_recv()

        def one(slot, _):
            zs = z_of(slot)
            near_x = pl.ds(xh * 2, 2)
            total = (
                kept[slot, near_x]
                + peer_in[slot, near_x].astype(F32)
                + far_in[slot].astype(F32)
            )
            grad_gate[:, zs] = (total * uder[slot]).astype(BF16)
            grad_up[:, zs] = (total * act[slot]).astype(BF16)
            return 0

        lax.fori_loop(first, first + n, one, 0)

    def partial_down(i, start, size):
        first, n = DOWN[i]
        cols = pl.ds(start, size)
        lhs = cbuf[pl.ds(first, n), :, :, :, cols].reshape(n * 256, size)
        rhs = hbuf[pl.ds(first, n)].reshape(n * 256, FF)
        out = lax.dot_general(lhs, rhs, (((0,), (0,)), ((), ())), preferred_element_type=F32)
        if i == 0:
            acc[cols, :] = out
        else:
            acc[cols, :] += out

    def down_round(i):
        @pl.loop(0, QD // TILE)
        def _(tile):
            partial_down(i, pl.multiple_of(tile * TILE, TILE), TILE)

    for j in range(2):
        arrive(1, j)
        ringed["first", j] = ring_first(j)
    pass_h(1)
    arrive_h(0)
    arrive_h(1)
    down_round(0)
    for j in range(2, 4):
        arrive(1, j)
        ringed["first", j] = ring_first(j)
    for copy in w_rest:
        copy.wait_recv()
    partial_hidden(0)
    pass_h(2)
    for j in range(4):
        arrive("first", j)
        ringed["last", 0, j] = ring_last(0, j)
    ringed["chunk", 1] = ring_chunk(1)
    ringed["chunk", 2] = ring_chunk(2)
    add_peer(0)
    partial_hidden(1)
    pass_h(3)
    send_far(0)
    send_far(1)
    add_peer(1)
    send_far(2)
    arrive("chunk", 1)
    ringed["last", 1] = ring_last(1)
    ringed["chunk", 3] = ring_chunk(3)
    arrive_h(2)
    down_round(1)
    arrive_h(3)

    def send_gd(k, src, dst, to, halves=None):
        at_rows = rows(*src)
        total = acc[at_rows, :]
        if halves is not None:
            total += halves[...].astype(F32)
        gd_out[at_rows] = total.astype(BF16)
        return send(gd_out.at[at_rows], dst, g_s.at[k], g_r.at[k], to)

    def half_of(k, half):
        return gd_in.at[k, pl.ds(half * HALF, HALF)]

    for j in range(4):
        arrive("last", 0, j)
    partial_down(2, *CHUNKS[0])
    up_far = send_gd(0, (2, 0), gd_half.at[0], upward)
    down_far = send_gd(1, (2, 1), gd_half.at[1], downward)
    arrive("chunk", 2)
    ringed["last", 2] = ring_last(2)
    partial_hidden(2, 0, CHUNKS[2][0])
    arrive("last", 1)
    partial_down(2, *CHUNKS[1])
    arrivals = [
        send_gd(2, (1, 1), half_of(0, 1), upward),
        send_gd(3, (3, 0), half_of(1, 0), downward),
    ]
    arrive("chunk", 3)
    ringed["last", 3] = ring_last(3)
    partial_hidden(2, CHUNKS[2][0], QD - CHUNKS[2][0])
    arrive("last", 2)
    partial_down(2, *CHUNKS[2])
    add_peer(2)
    send_far(3)
    up_far.wait_recv()
    arrivals.append(send_gd(4, (1, 0), half_of(0, 0), upward, gd_half.at[0]))
    down_far.wait_recv()
    arrivals.append(send_gd(5, (3, 1), half_of(1, 1), downward, gd_half.at[1]))
    partial_hidden(3, 0, CHUNKS[3][0])
    arrive("last", 3)
    partial_hidden(3, *CHUNKS[3])
    partial_down(2, *CHUNKS[3])
    add_peer(3)
    send_far(4)
    for i in range(5):
        finish_hidden(i)
    for copy in arrivals:
        copy.wait_recv()
    grad_down[...] = (
        acc[pl.ds(POS[0, 0], OWN), :] + gd_in[0].astype(F32) + gd_in[1].astype(F32)
    ).astype(BF16)
    for copy in started:
        copy.wait_send()


def write_out(*refs):
    copies = [
        pltpu.make_async_copy(refs[i], refs[3 + i], refs[6].at[i]) for i in range(3)
    ]
    for copy in copies:
        copy.start()
    for copy in copies:
        copy.wait()


def on_device(gate_pre, up_saved, cotangent, down_weight):
    vmem = pl.BlockSpec(memory_space=pltpu.VMEM)
    dma = pltpu.SemaphoreType.DMA
    tokens = (2, 8, ROWS, FF)
    shapes = (tokens, tokens, (OWN, FF))
    results = pl.pallas_call(
        kernel,
        name="ffn_down_backward",
        out_shape=tuple(pltpu.VMEM(shape, BF16) for shape in shapes),
        in_specs=[pl.BlockSpec(memory_space=pl.ANY)] * 4,
        out_specs=(vmem,) * 3,
        scratch_shapes=[
            pltpu.VMEM(tokens, BF16),
            pltpu.VMEM(tokens, BF16),
            pltpu.VMEM((ROWS, D), BF16),
            pltpu.VMEM((4, ROWS, QD), BF16),
            pltpu.VMEM((8, 2, 4, ROWS, QD), BF16),
            pltpu.VMEM((QD, FF), BF16),
            pltpu.VMEM((8, 2, 4, ROWS, FF), BF16),
            pltpu.VMEM((8, 2, ROWS, FF), F32),
            pltpu.VMEM((8, 2, ROWS, FF), F32),
            pltpu.VMEM((QD, FF), F32),
            pltpu.VMEM((8, 4, ROWS, FF), BF16),
            pltpu.VMEM((8, 4, ROWS, FF), BF16),
            pltpu.VMEM((8, 4, ROWS, FF), F32),
            pltpu.VMEM((3, 4, ROWS, FF), F32),
            pltpu.VMEM((8, 2, ROWS, FF), BF16),
            pltpu.VMEM((8, 2, ROWS, FF), BF16),
            pltpu.VMEM((QD, FF), BF16),
            pltpu.VMEM((2, HALF, FF), BF16),
            pltpu.VMEM((2, OWN, FF), BF16),
            dma((4,)), dma((7,)), dma((7,)),
            dma((2, 22)), dma((2, 22)),
            dma((6,)), dma((6,)),
            dma((3, 4)), dma((3, 4)),
            dma((4,)), dma((4,)),
            dma((5,)), dma((5,)),
            dma((6,)), dma((6,)),
        ],
        compiler_params=pltpu.CompilerParams(
            collective_id=0, has_side_effects=True, vmem_limit_bytes=52 << 20
        ),
        cost_estimate=pl.CostEstimate(
            flops=4 * 2048 * QD * FF, bytes_accessed=7 << 20, transcendentals=512 * FF
        ),
    )(
        gate_pre.reshape(tokens), up_saved.reshape(tokens), cotangent, down_weight
    )
    grad_gate, grad_up, grad_down = pl.pallas_call(
        write_out,
        name="write_out",
        out_shape=tuple(jax.ShapeDtypeStruct(shape, BF16) for shape in shapes),
        in_specs=[vmem] * 3,
        out_specs=(pl.BlockSpec(memory_space=pl.ANY),) * 3,
        scratch_shapes=[dma((3,))],
        compiler_params=pltpu.CompilerParams(vmem_limit_bytes=8 << 20),
    )(*[pltpu.with_memory_space_constraint(r, pltpu.VMEM) for r in results])
    return (grad_gate.reshape(512, FF), grad_up.reshape(512, FF), grad_down)


def solution(mesh):
    in_specs = (P("dp", "tensor"), P("dp", "tensor"), P(("dp", "tensor"), None), P("dp", "tensor"))
    out_specs = (P("dp", "tensor"), P("dp", "tensor"), P("dp", "tensor"))
    return jax.shard_map(
        on_device, mesh=mesh, in_specs=in_specs, out_specs=out_specs, check_vma=False
    )
```

```python
import functools

import jax
import jax.numpy as jnp
from jax import lax
from jax.experimental import pallas as pl
from jax.experimental.pallas import tpu as pltpu
from jax.sharding import PartitionSpec as P

MESH = pl.DeviceIdType.MESH
BF16, F32 = jnp.bfloat16, jnp.float32

root_coef = 0.7978845608028654
cubic_coef = 0.044715

D = 4608
FF = 1152
ROWS = 32
QD = 1152
OWN = 288
HALF = OWN // 2
TILE = 384
UNITS = ((2, 0), (2, 1), (1, 1), (3, 0), (1, 0), (3, 1), (0, 0), (0, 1))
POS = {unit: k * HALF for k, unit in enumerate(UNITS)}
SUBS = (0, 1, 3, 2)
ROUNDS = ((0, 3), (3, 2), (5, 2), (7, 1))
LATE = (3, 5)
CHUNKS = ((0, 384), (384, 256), (640, 256), (896, 256))
PARTS = ((0, 512), (512, 640))


def gelu_parts(gate_f32):
    inner = root_coef * (gate_f32 + cubic_coef * gate_f32 * gate_f32 * gate_f32)
    tanh_val = jnp.tanh(inner)
    activated = 0.5 * gate_f32 * (1.0 + tanh_val)
    derivative = 0.5 * (1.0 + tanh_val) + 0.5 * gate_f32 * (
        1.0 - tanh_val * tanh_val
    ) * root_coef * (1.0 + 3.0 * cubic_coef * gate_f32 * gate_f32)
    return (activated, derivative)


def kernel(
    gate_hbm, up_hbm, cot_hbm, weight, grad_gate, grad_up, grad_down,
    gate, up, cot, csrc, cbuf, wbuf, hbuf, act, uder, acc,
    peer_out, peer_in, kept, theirs_acc, far_out, far_in, gd_out, gd_half, gd_in,
    in_s, c_s, c_r, z_s, z_r, w_s, w_r, h_s, h_r, p_s, p_r, f_s, f_r, g_s, g_r,
):
    dp, tensor = lax.axis_index("dp"), lax.axis_index("tensor")
    y, xh, c = dp // 4, (dp // 2) % 2, dp % 2
    xl, z = tensor // 8, tensor % 8
    x = xh * 2 + xl

    def at(dx=0, dy=0, dz=0, dc=0):
        nx, ny, nz, nc = (x + dx) % 4, (y + dy) % 4, (z + dz) % 8, (c + dc) % 2
        return (ny * 4 + (nx // 2) * 2 + nc, (nx % 2) * 8 + nz)

    started = []

    def send(src, dst, ss, rs, to):
        copy = pltpu.make_async_remote_copy(
            src_ref=src, dst_ref=dst, send_sem=ss, recv_sem=rs, device_id=to, device_id_type=MESH
        )
        copy.start()
        started.append(copy)
        return copy

    near = [(dx, dc) for dx in range(4) for dc in range(2) if (dx, dc) != (0, 0)]
    barrier = pltpu.get_barrier_semaphore()
    partners = [at(dx=dx, dc=dc) for dx, dc in near] + [at(dz=1), at(dz=7), at(dy=1), at(dy=3)]
    for partner in partners:
        pl.semaphore_signal(barrier, inc=1, device_id=partner, device_id_type=MESH)

    def fetch(k, src, dst):
        copy = pltpu.make_async_copy(src, dst, in_s.at[k])
        copy.start()
        return copy

    cot_copy = fetch(0, cot_hbm, cot)
    weight_copy = fetch(1, weight, wbuf.at[pl.ds(POS[0, 0], OWN)])
    gate_copy = fetch(2, gate_hbm, gate)
    up_copy = fetch(3, up_hbm, up)
    cot_copy.wait()
    for (r, half), pos in POS.items():
        start = pl.multiple_of(((y + r) % 4) * QD, 128)
        block = cot[:, pl.ds(start, QD)]
        for q in range(4):
            first = q * OWN + half * HALF
            csrc[q, :, pos : pos + HALF] = block[:, first : first + HALF]
    cbuf[0, c, x] = csrc[xh * 2 + c]

    pl.semaphore_wait(barrier, len(partners))

    c_copies = {}

    def send_c(*dxs):
        for i, (dx, dc) in enumerate(near):
            if dx in dxs:
                nq = (((x + dx) % 4) // 2) * 2 + (c + dc) % 2
                c_copies[dx, dc] = send(
                    csrc.at[nq], cbuf.at[0, c, x], c_s.at[i], c_r.at[i], at(dx=dx, dc=dc)
                )

    send_c(0, 1, 3)

    def rows(r, half):
        return pl.ds(POS[r, half], HALF)

    def send_w(k, src, dst, to):
        return send(wbuf.at[rows(*src)], wbuf.at[rows(*dst)], w_s.at[k], w_r.at[k], to)

    upward, downward = at(dy=1), at(dy=3)
    weight_copy.wait()
    w_up = send_w(0, (0, 0), (3, 0), upward)
    w_down = send_w(1, (0, 1), (1, 1), downward)
    w_rest = [send_w(2, (0, 1), (3, 1), upward), send_w(3, (0, 0), (1, 0), downward)]

    def z_of(slot):
        return (z + (1 - 2 * (slot % 2)) * ((slot + 1) // 2) + 8) % 8

    def hidden(slot, _):
        zs = z_of(slot)
        up_f32 = up[:, zs].astype(F32)
        activated, derivative = gelu_parts(gate[:, zs].astype(F32))
        act[slot] = activated
        uder[slot] = up_f32 * derivative
        hbuf[slot, c, pl.ds(xh * 2, 2)] = (activated * up_f32).astype(BF16)
        return 0

    def send_z(way, k, src, dst):
        to = at(dz=1 if way == 0 else 7)
        return send(src, dst, z_s.at[way, k], z_r.at[way, k], to)

    def ring(j):
        xs = (x + SUBS[j]) % 4
        ringed[0, 0, j] = [
            send_z(way, j, cbuf.at[0, :, xs], cbuf.at[1 + way, :, xs]) for way in range(2)
        ]

    counter = [4]

    def ring_chunk(level, k, j=None):
        cols = pl.ds(*CHUNKS[k])
        xs = pl.ds(0, 4) if j is None else (x + SUBS[j]) % 4
        out = []
        for way in range(2):
            src, dst = 2 * level - 1 + way, 7 if level == 3 else 2 * level + 1 + way
            core = way if level == 3 else pl.ds(0, 2)
            out.append(
                send_z(
                    way, counter[0],
                    cbuf.at[src, core, xs, :, cols], cbuf.at[dst, core, xs, :, cols],
                )
            )
        counter[0] += 1
        ringed[level, k, j] = out

    ringed = {}

    def arrive(level, k, j=None):
        for copy in ringed[level, k, j]:
            copy.wait_recv()

    h_copies = {}

    def hidden_piece(i, from_xh):
        slots, cols = pl.ds(4 * (i % 2), 4), pl.ds(*PARTS[i // 2])
        return hbuf.at[slots, c, pl.ds(from_xh * 2, 2), :, cols]

    def send_h(i):
        mine = hidden_piece(i, xh)
        h_copies["p", i] = send(mine, mine, h_s.at[0, i], h_r.at[0, i], at(dc=1))
        h_copies["x", i] = send(mine, mine, h_s.at[1, i], h_r.at[1, i], at(dx=2))

    def pass_h(i):
        h_copies["x", i].wait_recv()
        theirs = hidden_piece(i, 1 - xh)
        h_copies["f", i] = send(theirs, theirs, h_s.at[2, i], h_r.at[2, i], at(dc=1))

    def arrive_h(i):
        h_copies["p", i].wait_recv()
        h_copies["f", i].wait_recv()

    gate_copy.wait()
    up_copy.wait()
    lax.fori_loop(0, 8, hidden, 0)
    for j in range(4):
        dx = (4 - SUBS[j]) % 4
        for dc in range(2):
            if (dx, dc) != (0, 0):
                c_copies[dx, dc].wait_recv()
        ring(j)
        if j == 2:
            send_c(2)
            for i in range(4):
                send_h(i)

    p_copies, f_copies = {}, {}

    def partial_hidden(i, start=0, size=QD):
        first, n = ROUNDS[i]
        begin, end = start == 0, start + size == QD
        cols = pl.ds(start, size)

        def one(slot, _):
            lhs = jnp.concatenate(
                [cbuf[slot, cp, :, :, cols].reshape(128, size) for cp in (1 - c, c)]
            )
            out = jnp.dot(lhs, wbuf[cols, :], preferred_element_type=F32)
            theirs, mine = out.reshape(2, 4, ROWS, FF)
            if not begin:
                theirs += theirs_acc[slot - LATE[0]]
                mine += kept[slot]
            kept[slot] = mine
            if end:
                peer_out[slot] = theirs.astype(BF16)
            else:
                theirs_acc[slot - LATE[0]] = theirs
            return 0

        lax.fori_loop(first, first + n, one, 0)
        if end:
            slots = pl.ds(first, n)
            p_copies[i] = send(
                peer_out.at[slots], peer_in.at[slots], p_s.at[i], p_r.at[i], at(dc=1)
            )

    def add_peer(i):
        first, n = ROUNDS[i]
        p_copies[i].wait_recv()

        def one(slot, _):
            far = pl.ds((1 - xh) * 2, 2)
            total = kept[slot, far] + peer_in[slot, far].astype(F32)
            far_out[slot] = total.astype(BF16)
            return 0

        lax.fori_loop(first, first + n, one, 0)

    def send_far(i):
        slots = pl.ds(*ROUNDS[i])
        f_copies[i] = send(
            far_out.at[slots], far_in.at[slots], f_s.at[i], f_r.at[i], at(dx=2)
        )

    def finish_hidden(i):
        first, n = ROUNDS[i]
        f_copies[i].wait_recv()

        def one(slot, _):
            zs = z_of(slot)
            near_x = pl.ds(xh * 2, 2)
            total = (
                kept[slot, near_x]
                + peer_in[slot, near_x].astype(F32)
                + far_in[slot].astype(F32)
            )
            grad_gate[:, zs] = (total * uder[slot]).astype(BF16)
            grad_up[:, zs] = (total * act[slot]).astype(BF16)
            return 0

        lax.fori_loop(first, first + n, one, 0)

    def partial_down(first, n, start, size, part):
        cols, units = pl.ds(start, size), pl.ds(*PARTS[part])
        lhs = cbuf[pl.ds(first, n), :, :, :, cols].reshape(n * 256, size)
        rhs = hbuf[pl.ds(first, n), :, :, :, units].reshape(n * 256, PARTS[part][1])
        out = lax.dot_general(lhs, rhs, (((0,), (0,)), ((), ())), preferred_element_type=F32)
        if first == 0:
            acc[cols, units] = out
        else:
            acc[cols, units] += out

    def early_down(part):
        @pl.loop(0, QD // TILE)
        def _(tile):
            partial_down(*ROUNDS[0], pl.multiple_of(tile * TILE, TILE), TILE, part)

    def late_down(k, part):
        partial_down(*LATE, *CHUNKS[k], part)

    gd = {}

    def send_gd(unit, part, way, dst, halves=None):
        at_rows, units = rows(*unit), pl.ds(*PARTS[part])
        total = acc[at_rows, units]
        if halves is not None:
            total += halves[:, units].astype(F32)
        gd_out[at_rows, units] = total.astype(BF16)
        k = len(gd)
        gd[unit, part] = send(
            gd_out.at[at_rows, units], dst.at[:, units],
            g_s.at[k], g_r.at[k], (upward, downward)[way],
        )

    def half_of(k, half):
        return gd_in.at[k, pl.ds(half * HALF, HALF)]

    def send_two(part):
        send_gd((2, 0), part, 0, gd_half.at[0])
        send_gd((2, 1), part, 1, gd_half.at[1])

    def send_one(part):
        send_gd((1, 1), part, 0, half_of(0, 1))
        send_gd((3, 0), part, 1, half_of(1, 0))

    def send_rest(part):
        gd[(2, 0), part].wait_recv()
        send_gd((1, 0), part, 0, half_of(0, 0), gd_half.at[0])
        gd[(2, 1), part].wait_recv()
        send_gd((3, 1), part, 1, half_of(1, 1), gd_half.at[1])

    for j in range(4):
        arrive(0, 0, j)
        ring_chunk(1, 0, j)
        if j == 2:
            w_up.wait_recv()
            w_rest.append(send_w(4, (3, 0), (2, 0), upward))
            w_down.wait_recv()
            w_rest.append(send_w(5, (1, 1), (2, 1), downward))
    pass_h(0)
    for j in range(4):
        arrive(1, 0, j)
        ring_chunk(2, 0, j)
    ring_chunk(1, 1)
    arrive_h(0)
    early_down(0)
    pass_h(1)
    for j in range(4):
        arrive(2, 0, j)
        ring_chunk(3, 0, j)
    for copy in w_rest:
        copy.wait_recv()
    partial_hidden(0)
    arrive(1, 1)
    ring_chunk(2, 1)
    ring_chunk(1, 2)
    pass_h(2)
    add_peer(0)
    send_far(0)
    arrive_h(1)
    for j in range(4):
        arrive(3, 0, j)
    late_down(0, 0)
    send_two(0)
    partial_hidden(1, 0, CHUNKS[2][0])
    arrive(2, 1)
    ring_chunk(3, 1)
    ring_chunk(1, 3)
    arrive_h(2)
    early_down(1)
    pass_h(3)
    arrive(1, 2)
    ring_chunk(2, 2)
    arrive(3, 1)
    late_down(1, 0)
    send_one(0)
    arrive_h(3)
    late_down(0, 1)
    send_two(1)
    late_down(1, 1)
    send_one(1)
    arrive(1, 3)
    ring_chunk(2, 3)
    partial_hidden(1, CHUNKS[2][0], QD - CHUNKS[2][0])
    arrive(2, 2)
    ring_chunk(3, 2)
    add_peer(1)
    send_far(1)
    partial_hidden(2, 0, CHUNKS[2][0])
    partial_hidden(3, 0, CHUNKS[2][0])
    arrive(2, 3)
    ring_chunk(3, 3)
    partial_hidden(2, CHUNKS[2][0], QD - CHUNKS[2][0])
    arrive(3, 2)
    late_down(2, 0)
    send_rest(0)
    late_down(2, 1)
    send_rest(1)
    add_peer(2)
    send_far(2)
    arrive(3, 3)
    partial_hidden(3, CHUNKS[2][0], QD - CHUNKS[2][0])
    late_down(3, 0)
    late_down(3, 1)
    add_peer(3)
    send_far(3)
    for i in range(4):
        finish_hidden(i)
    for part in range(2):
        for unit in ((1, 0), (1, 1), (3, 0), (3, 1)):
            gd[unit, part].wait_recv()
    grad_down[...] = (
        acc[pl.ds(POS[0, 0], OWN), :] + gd_in[0].astype(F32) + gd_in[1].astype(F32)
    ).astype(BF16)
    for copy in started:
        copy.wait_send()


def write_out(*refs):
    copies = [
        pltpu.make_async_copy(refs[i], refs[3 + i], refs[6].at[i]) for i in range(3)
    ]
    for copy in copies:
        copy.start()
    for copy in copies:
        copy.wait()


def on_device(gate_pre, up_saved, cotangent, down_weight):
    vmem = pl.BlockSpec(memory_space=pltpu.VMEM)
    dma = pltpu.SemaphoreType.DMA
    tokens = (2, 8, ROWS, FF)
    shapes = (tokens, tokens, (OWN, FF))
    results = pl.pallas_call(
        kernel,
        name="ffn_down_backward",
        out_shape=tuple(pltpu.VMEM(shape, BF16) for shape in shapes),
        in_specs=[pl.BlockSpec(memory_space=pl.ANY)] * 4,
        out_specs=(vmem,) * 3,
        scratch_shapes=[
            pltpu.VMEM(tokens, BF16),
            pltpu.VMEM(tokens, BF16),
            pltpu.VMEM((ROWS, D), BF16),
            pltpu.VMEM((4, ROWS, QD), BF16),
            pltpu.VMEM((8, 2, 4, ROWS, QD), BF16),
            pltpu.VMEM((QD, FF), BF16),
            pltpu.VMEM((8, 2, 4, ROWS, FF), BF16),
            pltpu.VMEM((8, 2, ROWS, FF), F32),
            pltpu.VMEM((8, 2, ROWS, FF), F32),
            pltpu.VMEM((QD, FF), F32),
            pltpu.VMEM((8, 4, ROWS, FF), BF16),
            pltpu.VMEM((8, 4, ROWS, FF), BF16),
            pltpu.VMEM((8, 4, ROWS, FF), F32),
            pltpu.VMEM((LATE[1], 4, ROWS, FF), F32),
            pltpu.VMEM((8, 2, ROWS, FF), BF16),
            pltpu.VMEM((8, 2, ROWS, FF), BF16),
            pltpu.VMEM((QD, FF), BF16),
            pltpu.VMEM((2, HALF, FF), BF16),
            pltpu.VMEM((2, OWN, FF), BF16),
            dma((4,)), dma((7,)), dma((7,)),
            dma((2, 25)), dma((2, 25)),
            dma((6,)), dma((6,)),
            dma((3, 4)), dma((3, 4)),
            dma((4,)), dma((4,)),
            dma((4,)), dma((4,)),
            dma((12,)), dma((12,)),
        ],
        compiler_params=pltpu.CompilerParams(
            collective_id=0, has_side_effects=True, vmem_limit_bytes=52 << 20
        ),
        cost_estimate=pl.CostEstimate(
            flops=4 * 2048 * QD * FF, bytes_accessed=7 << 20, transcendentals=512 * FF
        ),
    )(
        gate_pre.reshape(tokens), up_saved.reshape(tokens), cotangent, down_weight
    )
    grad_gate, grad_up, grad_down = pl.pallas_call(
        write_out,
        name="write_out",
        out_shape=tuple(jax.ShapeDtypeStruct(shape, BF16) for shape in shapes),
        in_specs=[vmem] * 3,
        out_specs=(pl.BlockSpec(memory_space=pl.ANY),) * 3,
        scratch_shapes=[dma((3,))],
        compiler_params=pltpu.CompilerParams(vmem_limit_bytes=8 << 20),
    )(*[pltpu.with_memory_space_constraint(r, pltpu.VMEM) for r in results])
    return (grad_gate.reshape(512, FF), grad_up.reshape(512, FF), grad_down)


def solution(mesh):
    in_specs = (P("dp", "tensor"), P("dp", "tensor"), P(("dp", "tensor"), None), P("dp", "tensor"))
    out_specs = (P("dp", "tensor"), P("dp", "tensor"), P("dp", "tensor"))
    return jax.shard_map(
        on_device, mesh=mesh, in_specs=in_specs, out_specs=out_specs, check_vma=False
    )
```

```python
import functools

import jax
import jax.numpy as jnp
from jax import lax
from jax.experimental import pallas as pl
from jax.experimental.pallas import tpu as pltpu
from jax.sharding import PartitionSpec as P

MESH = pl.DeviceIdType.MESH
BF16, F32 = jnp.bfloat16, jnp.float32

root_coef = 0.7978845608028654
cubic_coef = 0.044715

D = 4608
FF = 1152
ROWS = 32
QD = 1152
OWN = 288
HALF = OWN // 2
TILE = 384
UNITS = ((2, 0), (2, 1), (1, 1), (3, 0), (1, 0), (3, 1), (0, 0), (0, 1))
POS = {unit: k * HALF for k, unit in enumerate(UNITS)}
SUBS = (0, 1, 3, 2)
ROUNDS = ((0, 3), (3, 2), (5, 2), (7, 1))
LATE = (3, 5)
CHUNKS = ((0, 384), (384, 256), (640, 256), (896, 256))
PARTS = ((0, 512), (512, 640))


def gelu_parts(gate_f32):
    inner = root_coef * (gate_f32 + cubic_coef * gate_f32 * gate_f32 * gate_f32)
    tanh_val = jnp.tanh(inner)
    activated = 0.5 * gate_f32 * (1.0 + tanh_val)
    derivative = 0.5 * (1.0 + tanh_val) + 0.5 * gate_f32 * (
        1.0 - tanh_val * tanh_val
    ) * root_coef * (1.0 + 3.0 * cubic_coef * gate_f32 * gate_f32)
    return (activated, derivative)


def kernel(
    gate_hbm, up_hbm, cot_hbm, weight, grad_gate, grad_up, grad_down,
    gate, up, cot, csrc, cbuf, wbuf, hbuf, act, uder, acc,
    peer_out, peer_in, kept, theirs_acc, far_out, far_in, gd_out, gd_half, gd_in,
    in_s, c_s, c_r, z_s, z_r, w_s, w_r, h_s, h_r, p_s, p_r, f_s, f_r, g_s, g_r,
):
    dp, tensor = lax.axis_index("dp"), lax.axis_index("tensor")
    y, xh, c = dp // 4, (dp // 2) % 2, dp % 2
    xl, z = tensor // 8, tensor % 8
    x = xh * 2 + xl

    def at(dx=0, dy=0, dz=0, dc=0):
        nx, ny, nz, nc = (x + dx) % 4, (y + dy) % 4, (z + dz) % 8, (c + dc) % 2
        return (ny * 4 + (nx // 2) * 2 + nc, (nx % 2) * 8 + nz)

    started = []

    def send(src, dst, ss, rs, to):
        copy = pltpu.make_async_remote_copy(
            src_ref=src, dst_ref=dst, send_sem=ss, recv_sem=rs, device_id=to, device_id_type=MESH
        )
        copy.start()
        started.append(copy)
        return copy

    near = [(dx, dc) for dx in range(4) for dc in range(2) if (dx, dc) != (0, 0)]
    barrier = pltpu.get_barrier_semaphore()
    partners = [at(dx=dx, dc=dc) for dx, dc in near] + [at(dz=1), at(dz=7), at(dy=1), at(dy=3)]
    for partner in partners:
        pl.semaphore_signal(barrier, inc=1, device_id=partner, device_id_type=MESH)

    def fetch(k, src, dst):
        copy = pltpu.make_async_copy(src, dst, in_s.at[k])
        copy.start()
        return copy

    cot_copy = fetch(0, cot_hbm, cot)
    weight_copy = fetch(1, weight, wbuf.at[pl.ds(POS[0, 0], OWN)])
    gate_copy = fetch(2, gate_hbm, gate)
    up_copy = fetch(3, up_hbm, up)
    cot_copy.wait()
    for (r, half), pos in POS.items():
        start = pl.multiple_of(((y + r) % 4) * QD, 128)
        block = cot[:, pl.ds(start, QD)]
        for q in range(4):
            first = q * OWN + half * HALF
            csrc[q, :, pos : pos + HALF] = block[:, first : first + HALF]
    cbuf[0, c, x] = csrc[xh * 2 + c]

    pl.semaphore_wait(barrier, len(partners))

    c_copies = {}

    def send_c(*dxs):
        for i, (dx, dc) in enumerate(near):
            if dx in dxs:
                nq = (((x + dx) % 4) // 2) * 2 + (c + dc) % 2
                c_copies[dx, dc] = send(
                    csrc.at[nq], cbuf.at[0, c, x], c_s.at[i], c_r.at[i], at(dx=dx, dc=dc)
                )

    send_c(0, 1, 3)

    def rows(r, half):
        return pl.ds(POS[r, half], HALF)

    def send_w(k, src, dst, to):
        return send(wbuf.at[rows(*src)], wbuf.at[rows(*dst)], w_s.at[k], w_r.at[k], to)

    upward, downward = at(dy=1), at(dy=3)
    weight_copy.wait()
    w_up = send_w(0, (0, 0), (3, 0), upward)
    w_down = send_w(1, (0, 1), (1, 1), downward)
    w_rest = [send_w(2, (0, 1), (3, 1), upward), send_w(3, (0, 0), (1, 0), downward)]

    def z_of(slot):
        return (z + (1 - 2 * (slot % 2)) * ((slot + 1) // 2) + 8) % 8

    def hidden(slot, _):
        zs = z_of(slot)
        up_f32 = up[:, zs].astype(F32)
        activated, derivative = gelu_parts(gate[:, zs].astype(F32))
        act[slot] = activated
        uder[slot] = up_f32 * derivative
        hbuf[slot, c, pl.ds(xh * 2, 2)] = (activated * up_f32).astype(BF16)
        return 0

    def send_z(way, k, src, dst):
        to = at(dz=1 if way == 0 else 7)
        return send(src, dst, z_s.at[way, k], z_r.at[way, k], to)

    def ring(j):
        xs = (x + SUBS[j]) % 4
        ringed[0, 0, j] = [
            send_z(way, j, cbuf.at[0, :, xs], cbuf.at[1 + way, :, xs]) for way in range(2)
        ]

    counter = [4]

    def ring_chunk(level, k, j=None):
        cols = pl.ds(*CHUNKS[k])
        xs = pl.ds(0, 4) if j is None else (x + SUBS[j]) % 4
        out = []
        for way in range(2):
            src, dst = 2 * level - 1 + way, 7 if level == 3 else 2 * level + 1 + way
            core = way if level == 3 else pl.ds(0, 2)
            out.append(
                send_z(
                    way, counter[0],
                    cbuf.at[src, core, xs, :, cols], cbuf.at[dst, core, xs, :, cols],
                )
            )
        counter[0] += 1
        ringed[level, k, j] = out

    ringed = {}

    def arrive(level, k, j=None):
        for copy in ringed[level, k, j]:
            copy.wait_recv()

    h_copies = {}

    def hidden_piece(i, from_xh):
        slots, cols = pl.ds(4 * (i % 2), 4), pl.ds(*PARTS[i // 2])
        return hbuf.at[slots, c, pl.ds(from_xh * 2, 2), :, cols]

    def send_h(i):
        mine = hidden_piece(i, xh)
        h_copies["p", i] = send(mine, mine, h_s.at[0, i], h_r.at[0, i], at(dc=1))
        h_copies["x", i] = send(mine, mine, h_s.at[1, i], h_r.at[1, i], at(dx=2))

    def pass_h(i):
        h_copies["x", i].wait_recv()
        theirs = hidden_piece(i, 1 - xh)
        h_copies["f", i] = send(theirs, theirs, h_s.at[2, i], h_r.at[2, i], at(dc=1))

    def arrive_h(i):
        h_copies["p", i].wait_recv()
        h_copies["f", i].wait_recv()

    gate_copy.wait()
    up_copy.wait()
    lax.fori_loop(0, 8, hidden, 0)
    for j in range(4):
        dx = (4 - SUBS[j]) % 4
        for dc in range(2):
            if (dx, dc) != (0, 0):
                c_copies[dx, dc].wait_recv()
        ring(j)
        if j == 2:
            send_c(2)
            for i in range(4):
                send_h(i)

    p_copies, f_copies = {}, {}

    def partial_hidden(i, start=0, size=QD):
        first, n = ROUNDS[i]
        begin, end = start == 0, start + size == QD
        cols = pl.ds(start, size)

        def one(slot, _):
            lhs = jnp.concatenate(
                [cbuf[slot, cp, :, :, cols].reshape(128, size) for cp in (1 - c, c)]
            )
            out = jnp.dot(lhs, wbuf[cols, :], preferred_element_type=F32)
            theirs, mine = out.reshape(2, 4, ROWS, FF)
            if not begin:
                theirs += theirs_acc[slot - LATE[0]]
                mine += kept[slot]
            kept[slot] = mine
            if end:
                peer_out[slot] = theirs.astype(BF16)
            else:
                theirs_acc[slot - LATE[0]] = theirs
            return 0

        lax.fori_loop(first, first + n, one, 0)
        if end:
            slots = pl.ds(first, n)
            p_copies[i] = send(
                peer_out.at[slots], peer_in.at[slots], p_s.at[i], p_r.at[i], at(dc=1)
            )

    def add_peer(i):
        first, n = ROUNDS[i]
        p_copies[i].wait_recv()

        def one(slot, _):
            far = pl.ds((1 - xh) * 2, 2)
            total = kept[slot, far] + peer_in[slot, far].astype(F32)
            far_out[slot] = total.astype(BF16)
            return 0

        lax.fori_loop(first, first + n, one, 0)

    def send_far(i):
        slots = pl.ds(*ROUNDS[i])
        f_copies[i] = send(
            far_out.at[slots], far_in.at[slots], f_s.at[i], f_r.at[i], at(dx=2)
        )

    def finish_hidden(i):
        first, n = ROUNDS[i]
        f_copies[i].wait_recv()

        def one(slot, _):
            zs = z_of(slot)
            near_x = pl.ds(xh * 2, 2)
            total = (
                kept[slot, near_x]
                + peer_in[slot, near_x].astype(F32)
                + far_in[slot].astype(F32)
            )
            grad_gate[:, zs] = (total * uder[slot]).astype(BF16)
            grad_up[:, zs] = (total * act[slot]).astype(BF16)
            return 0

        lax.fori_loop(first, first + n, one, 0)

    def partial_down(first, n, start, size, part):
        cols, units = pl.ds(start, size), pl.ds(*PARTS[part])
        lhs = cbuf[pl.ds(first, n), :, :, :, cols].reshape(n * 256, size)
        rhs = hbuf[pl.ds(first, n), :, :, :, units].reshape(n * 256, PARTS[part][1])
        out = lax.dot_general(lhs, rhs, (((0,), (0,)), ((), ())), preferred_element_type=F32)
        if first == 0:
            acc[cols, units] = out
        else:
            acc[cols, units] += out

    def early_down(part):
        @pl.loop(0, QD // TILE)
        def _(tile):
            partial_down(*ROUNDS[0], pl.multiple_of(tile * TILE, TILE), TILE, part)

    def late_down(k, part):
        partial_down(*LATE, *CHUNKS[k], part)

    gd = {}

    def send_gd(unit, part, way, dst, halves=None):
        at_rows, units = rows(*unit), pl.ds(*PARTS[part])
        total = acc[at_rows, units]
        if halves is not None:
            total += halves[:, units].astype(F32)
        gd_out[at_rows, units] = total.astype(BF16)
        k = len(gd)
        gd[unit, part] = send(
            gd_out.at[at_rows, units], dst.at[:, units],
            g_s.at[k], g_r.at[k], (upward, downward)[way],
        )

    def half_of(k, half):
        return gd_in.at[k, pl.ds(half * HALF, HALF)]

    def send_two(part):
        send_gd((2, 0), part, 0, gd_half.at[0])
        send_gd((2, 1), part, 1, gd_half.at[1])

    def send_one(part):
        send_gd((1, 1), part, 0, half_of(0, 1))
        send_gd((3, 0), part, 1, half_of(1, 0))

    def send_rest(part):
        gd[(2, 0), part].wait_recv()
        send_gd((1, 0), part, 0, half_of(0, 0), gd_half.at[0])
        gd[(2, 1), part].wait_recv()
        send_gd((3, 1), part, 1, half_of(1, 1), gd_half.at[1])

    for j in range(4):
        arrive(0, 0, j)
        ring_chunk(1, 0, j)
        if j == 2:
            w_up.wait_recv()
            w_rest.append(send_w(4, (3, 0), (2, 0), upward))
            w_down.wait_recv()
            w_rest.append(send_w(5, (1, 1), (2, 1), downward))
    pass_h(0)
    for j in range(4):
        arrive(1, 0, j)
        ring_chunk(2, 0, j)
    ring_chunk(1, 1)
    arrive_h(0)
    early_down(0)
    pass_h(1)
    for j in range(4):
        arrive(2, 0, j)
        ring_chunk(3, 0, j)
    for copy in w_rest:
        copy.wait_recv()
    partial_hidden(0)
    arrive(1, 1)
    ring_chunk(2, 1)
    ring_chunk(1, 2)
    pass_h(2)
    add_peer(0)
    send_far(0)
    arrive_h(1)
    for j in range(4):
        arrive(3, 0, j)
    late_down(0, 0)
    send_two(0)
    partial_hidden(1, 0, CHUNKS[2][0])
    arrive(2, 1)
    ring_chunk(1, 3)
    ring_chunk(3, 1)
    arrive_h(2)
    early_down(1)
    pass_h(3)
    arrive(1, 2)
    ring_chunk(2, 2)
    partial_hidden(1, *CHUNKS[2])
    arrive_h(3)
    late_down(0, 1)
    send_two(1)
    arrive(1, 3)
    ring_chunk(2, 3)
    partial_hidden(1, *CHUNKS[3])
    arrive(3, 1)
    late_down(1, 0)
    add_peer(1)
    send_far(1)
    send_one(0)
    late_down(1, 1)
    send_one(1)
    partial_hidden(2, 0, CHUNKS[2][0])
    arrive(2, 2)
    ring_chunk(3, 2)
    partial_hidden(2, *CHUNKS[2])
    partial_hidden(3, 0, CHUNKS[2][0])
    arrive(2, 3)
    ring_chunk(3, 3)
    partial_hidden(2, *CHUNKS[3])
    add_peer(2)
    send_far(2)
    arrive(3, 2)
    late_down(2, 0)
    send_rest(0)
    late_down(2, 1)
    send_rest(1)
    arrive(3, 3)
    partial_hidden(3, CHUNKS[2][0], QD - CHUNKS[2][0])
    late_down(3, 0)
    add_peer(3)
    send_far(3)
    late_down(3, 1)
    for i in range(3):
        finish_hidden(i)
    for part in range(2):
        for unit in ((1, 0), (1, 1), (3, 0), (3, 1)):
            gd[unit, part].wait_recv()
    grad_down[...] = (
        acc[pl.ds(POS[0, 0], OWN), :] + gd_in[0].astype(F32) + gd_in[1].astype(F32)
    ).astype(BF16)
    finish_hidden(3)
    for copy in started:
        copy.wait_send()


def write_out(*refs):
    copies = [
        pltpu.make_async_copy(refs[i], refs[3 + i], refs[6].at[i]) for i in range(3)
    ]
    for copy in copies:
        copy.start()
    for copy in copies:
        copy.wait()


def on_device(gate_pre, up_saved, cotangent, down_weight):
    vmem = pl.BlockSpec(memory_space=pltpu.VMEM)
    dma = pltpu.SemaphoreType.DMA
    tokens = (2, 8, ROWS, FF)
    shapes = (tokens, tokens, (OWN, FF))
    results = pl.pallas_call(
        kernel,
        name="ffn_down_backward",
        out_shape=tuple(pltpu.VMEM(shape, BF16) for shape in shapes),
        in_specs=[pl.BlockSpec(memory_space=pl.ANY)] * 4,
        out_specs=(vmem,) * 3,
        scratch_shapes=[
            pltpu.VMEM(tokens, BF16),
            pltpu.VMEM(tokens, BF16),
            pltpu.VMEM((ROWS, D), BF16),
            pltpu.VMEM((4, ROWS, QD), BF16),
            pltpu.VMEM((8, 2, 4, ROWS, QD), BF16),
            pltpu.VMEM((QD, FF), BF16),
            pltpu.VMEM((8, 2, 4, ROWS, FF), BF16),
            pltpu.VMEM((8, 2, ROWS, FF), F32),
            pltpu.VMEM((8, 2, ROWS, FF), F32),
            pltpu.VMEM((QD, FF), F32),
            pltpu.VMEM((8, 4, ROWS, FF), BF16),
            pltpu.VMEM((8, 4, ROWS, FF), BF16),
            pltpu.VMEM((8, 4, ROWS, FF), F32),
            pltpu.VMEM((LATE[1], 4, ROWS, FF), F32),
            pltpu.VMEM((8, 2, ROWS, FF), BF16),
            pltpu.VMEM((8, 2, ROWS, FF), BF16),
            pltpu.VMEM((QD, FF), BF16),
            pltpu.VMEM((2, HALF, FF), BF16),
            pltpu.VMEM((2, OWN, FF), BF16),
            dma((4,)), dma((7,)), dma((7,)),
            dma((2, 25)), dma((2, 25)),
            dma((6,)), dma((6,)),
            dma((3, 4)), dma((3, 4)),
            dma((4,)), dma((4,)),
            dma((4,)), dma((4,)),
            dma((12,)), dma((12,)),
        ],
        compiler_params=pltpu.CompilerParams(
            collective_id=0, has_side_effects=True, vmem_limit_bytes=52 << 20
        ),
        cost_estimate=pl.CostEstimate(
            flops=4 * 2048 * QD * FF, bytes_accessed=7 << 20, transcendentals=512 * FF
        ),
    )(
        gate_pre.reshape(tokens), up_saved.reshape(tokens), cotangent, down_weight
    )
    grad_gate, grad_up, grad_down = pl.pallas_call(
        write_out,
        name="write_out",
        out_shape=tuple(jax.ShapeDtypeStruct(shape, BF16) for shape in shapes),
        in_specs=[vmem] * 3,
        out_specs=(pl.BlockSpec(memory_space=pl.ANY),) * 3,
        scratch_shapes=[dma((3,))],
        compiler_params=pltpu.CompilerParams(vmem_limit_bytes=8 << 20),
    )(*[pltpu.with_memory_space_constraint(r, pltpu.VMEM) for r in results])
    return (grad_gate.reshape(512, FF), grad_up.reshape(512, FF), grad_down)


def solution(mesh):
    in_specs = (P("dp", "tensor"), P("dp", "tensor"), P(("dp", "tensor"), None), P("dp", "tensor"))
    out_specs = (P("dp", "tensor"), P("dp", "tensor"), P("dp", "tensor"))
    return jax.shard_map(
        on_device, mesh=mesh, in_specs=in_specs, out_specs=out_specs, check_vma=False
    )
```

```python
import functools

import jax
import jax.numpy as jnp
from jax import lax
from jax.experimental import pallas as pl
from jax.experimental.pallas import tpu as pltpu
from jax.sharding import PartitionSpec as P

MESH = pl.DeviceIdType.MESH
BF16, F32 = jnp.bfloat16, jnp.float32

root_coef = 0.7978845608028654
cubic_coef = 0.044715

D = 4608
FF = 1152
ROWS = 32
QD = 1152
OWN = 288
HALF = OWN // 2
TILE = 384
UNITS = ((2, 0), (2, 1), (1, 1), (3, 0), (1, 0), (3, 1), (0, 0), (0, 1))
POS = {unit: k * HALF for k, unit in enumerate(UNITS)}
SUBS = (0, 1, 3, 2)
ROUNDS = ((0, 3), (3, 2), (5, 2), (7, 1))
LATE = (3, 5)
CHUNKS = ((0, 384), (384, 256), (640, 256), (896, 256))
PARTS = ((0, 512), (512, 640))


def gelu_parts(gate_f32):
    inner = root_coef * (gate_f32 + cubic_coef * gate_f32 * gate_f32 * gate_f32)
    tanh_val = jnp.tanh(inner)
    activated = 0.5 * gate_f32 * (1.0 + tanh_val)
    derivative = 0.5 * (1.0 + tanh_val) + 0.5 * gate_f32 * (
        1.0 - tanh_val * tanh_val
    ) * root_coef * (1.0 + 3.0 * cubic_coef * gate_f32 * gate_f32)
    return (activated, derivative)


def kernel(
    gate_hbm, up_hbm, cot_hbm, weight, grad_gate, grad_up, grad_down,
    gate, up, cot, csrc, cbuf, wbuf, hbuf, act, uder, acc,
    peer_out, peer_in, kept, theirs_acc, far_out, far_in, gd_out, gd_half, gd_in,
    in_s, c_s, c_r, z_s, z_r, w_s, w_r, h_s, h_r, p_s, p_r, f_s, f_r, g_s, g_r,
):
    dp, tensor = lax.axis_index("dp"), lax.axis_index("tensor")
    y, xh, c = dp // 4, (dp // 2) % 2, dp % 2
    xl, z = tensor // 8, tensor % 8
    x = xh * 2 + xl

    def at(dx=0, dy=0, dz=0, dc=0):
        nx, ny, nz, nc = (x + dx) % 4, (y + dy) % 4, (z + dz) % 8, (c + dc) % 2
        return (ny * 4 + (nx // 2) * 2 + nc, (nx % 2) * 8 + nz)

    started = []

    def send(src, dst, ss, rs, to):
        copy = pltpu.make_async_remote_copy(
            src_ref=src, dst_ref=dst, send_sem=ss, recv_sem=rs, device_id=to, device_id_type=MESH
        )
        copy.start()
        started.append(copy)
        return copy

    near = [(dx, dc) for dx in range(4) for dc in range(2) if (dx, dc) != (0, 0)]
    barrier = pltpu.get_barrier_semaphore()
    partners = [at(dx=dx, dc=dc) for dx, dc in near] + [at(dz=1), at(dz=7), at(dy=1), at(dy=3)]
    for partner in partners:
        pl.semaphore_signal(barrier, inc=1, device_id=partner, device_id_type=MESH)

    def fetch(k, src, dst):
        copy = pltpu.make_async_copy(src, dst, in_s.at[k])
        copy.start()
        return copy

    cot_copy = fetch(0, cot_hbm, cot)
    weight_copy = fetch(1, weight, wbuf.at[pl.ds(POS[0, 0], OWN)])
    gate_copy = fetch(2, gate_hbm, gate)
    up_copy = fetch(3, up_hbm, up)
    cot_copy.wait()
    for (r, half), pos in POS.items():
        start = pl.multiple_of(((y + r) % 4) * QD, 128)
        block = cot[:, pl.ds(start, QD)]
        for q in range(4):
            first = q * OWN + half * HALF
            csrc[q, :, pos : pos + HALF] = block[:, first : first + HALF]
    cbuf[0, c, x] = csrc[xh * 2 + c]

    pl.semaphore_wait(barrier, len(partners))

    c_copies = {}

    def send_c(*dxs):
        for i, (dx, dc) in enumerate(near):
            if dx in dxs:
                nq = (((x + dx) % 4) // 2) * 2 + (c + dc) % 2
                c_copies[dx, dc] = send(
                    csrc.at[nq], cbuf.at[0, c, x], c_s.at[i], c_r.at[i], at(dx=dx, dc=dc)
                )

    send_c(0, 1, 3)

    def rows(r, half):
        return pl.ds(POS[r, half], HALF)

    def send_w(k, src, dst, to):
        return send(wbuf.at[rows(*src)], wbuf.at[rows(*dst)], w_s.at[k], w_r.at[k], to)

    upward, downward = at(dy=1), at(dy=3)
    weight_copy.wait()
    w_up = send_w(0, (0, 0), (3, 0), upward)
    w_down = send_w(1, (0, 1), (1, 1), downward)
    w_rest = [send_w(2, (0, 1), (3, 1), upward), send_w(3, (0, 0), (1, 0), downward)]

    def z_of(slot):
        return (z + (1 - 2 * (slot % 2)) * ((slot + 1) // 2) + 8) % 8

    def hidden(slot, _):
        zs = z_of(slot)
        up_f32 = up[:, zs].astype(F32)
        activated, derivative = gelu_parts(gate[:, zs].astype(F32))
        act[slot] = activated
        uder[slot] = up_f32 * derivative
        hbuf[slot, c, pl.ds(xh * 2, 2)] = (activated * up_f32).astype(BF16)
        return 0

    def send_z(way, k, src, dst):
        to = at(dz=1 if way == 0 else 7)
        return send(src, dst, z_s.at[way, k], z_r.at[way, k], to)

    def ring(j):
        xs = (x + SUBS[j]) % 4
        ringed[0, 0, j] = [
            send_z(way, j, cbuf.at[0, :, xs], cbuf.at[1 + way, :, xs]) for way in range(2)
        ]

    counter = [4]

    def ring_chunk(level, k, j=None):
        cols = pl.ds(*CHUNKS[k])
        xs = pl.ds(0, 4) if j is None else (x + SUBS[j]) % 4
        out = []
        for way in range(2):
            src, dst = 2 * level - 1 + way, 7 if level == 3 else 2 * level + 1 + way
            core = way if level == 3 else pl.ds(0, 2)
            out.append(
                send_z(
                    way, counter[0],
                    cbuf.at[src, core, xs, :, cols], cbuf.at[dst, core, xs, :, cols],
                )
            )
        counter[0] += 1
        ringed[level, k, j] = out

    ringed = {}

    def arrive(level, k, j=None):
        for copy in ringed[level, k, j]:
            copy.wait_recv()

    h_copies = {}

    def hidden_piece(i, from_xh):
        slots, cols = pl.ds(4 * (i % 2), 4), pl.ds(*PARTS[i // 2])
        return hbuf.at[slots, c, pl.ds(from_xh * 2, 2), :, cols]

    def send_h(i):
        mine = hidden_piece(i, xh)
        h_copies["p", i] = send(mine, mine, h_s.at[0, i], h_r.at[0, i], at(dc=1))
        h_copies["x", i] = send(mine, mine, h_s.at[1, i], h_r.at[1, i], at(dx=2))

    def pass_h(i):
        h_copies["x", i].wait_recv()
        theirs = hidden_piece(i, 1 - xh)
        h_copies["f", i] = send(theirs, theirs, h_s.at[2, i], h_r.at[2, i], at(dc=1))

    def arrive_h(i):
        h_copies["p", i].wait_recv()
        h_copies["f", i].wait_recv()

    for j in range(4):
        dx = (4 - SUBS[j]) % 4
        for dc in range(2):
            if (dx, dc) != (0, 0):
                c_copies[dx, dc].wait_recv()
        ring(j)
        if j == 0:
            gate_copy.wait()
            up_copy.wait()
            lax.fori_loop(0, 8, hidden, 0)
        if j == 2:
            send_c(2)
            for i in range(4):
                send_h(i)

    p_copies, f_copies = {}, {}

    def partial_hidden(i, start=0, size=QD):
        first, n = ROUNDS[i]
        begin, end = start == 0, start + size == QD
        cols = pl.ds(start, size)

        def one(slot, _):
            lhs = jnp.concatenate(
                [cbuf[slot, cp, :, :, cols].reshape(128, size) for cp in (1 - c, c)]
            )
            out = jnp.dot(lhs, wbuf[cols, :], preferred_element_type=F32)
            theirs, mine = out.reshape(2, 4, ROWS, FF)
            if not begin:
                theirs += theirs_acc[slot - LATE[0]]
                mine += kept[slot]
            kept[slot] = mine
            if end:
                peer_out[slot] = theirs.astype(BF16)
            else:
                theirs_acc[slot - LATE[0]] = theirs
            return 0

        lax.fori_loop(first, first + n, one, 0)
        if end:
            slots = pl.ds(first, n)
            p_copies[i] = send(
                peer_out.at[slots], peer_in.at[slots], p_s.at[i], p_r.at[i], at(dc=1)
            )

    def add_peer(i):
        first, n = ROUNDS[i]
        p_copies[i].wait_recv()

        def one(slot, _):
            far = pl.ds((1 - xh) * 2, 2)
            total = kept[slot, far] + peer_in[slot, far].astype(F32)
            far_out[slot] = total.astype(BF16)
            return 0

        lax.fori_loop(first, first + n, one, 0)

    def send_far(i):
        slots = pl.ds(*ROUNDS[i])
        f_copies[i] = send(
            far_out.at[slots], far_in.at[slots], f_s.at[i], f_r.at[i], at(dx=2)
        )

    def finish_hidden(i):
        first, n = ROUNDS[i]
        f_copies[i].wait_recv()

        def one(slot, _):
            zs = z_of(slot)
            near_x = pl.ds(xh * 2, 2)
            total = (
                kept[slot, near_x]
                + peer_in[slot, near_x].astype(F32)
                + far_in[slot].astype(F32)
            )
            grad_gate[:, zs] = (total * uder[slot]).astype(BF16)
            grad_up[:, zs] = (total * act[slot]).astype(BF16)
            return 0

        lax.fori_loop(first, first + n, one, 0)

    def partial_down(first, n, start, size, part):
        cols, units = pl.ds(start, size), pl.ds(*PARTS[part])
        lhs = cbuf[pl.ds(first, n), :, :, :, cols].reshape(n * 256, size)
        rhs = hbuf[pl.ds(first, n), :, :, :, units].reshape(n * 256, PARTS[part][1])
        out = lax.dot_general(lhs, rhs, (((0,), (0,)), ((), ())), preferred_element_type=F32)
        if first == 0:
            acc[cols, units] = out
        else:
            acc[cols, units] += out

    def early_down(part):
        @pl.loop(0, QD // TILE)
        def _(tile):
            partial_down(*ROUNDS[0], pl.multiple_of(tile * TILE, TILE), TILE, part)

    def late_down(k, part):
        partial_down(*LATE, *CHUNKS[k], part)

    gd = {}

    def send_gd(unit, part, way, dst, halves=None):
        at_rows, units = rows(*unit), pl.ds(*PARTS[part])
        total = acc[at_rows, units]
        if halves is not None:
            total += halves[:, units].astype(F32)
        gd_out[at_rows, units] = total.astype(BF16)
        k = len(gd)
        gd[unit, part] = send(
            gd_out.at[at_rows, units], dst.at[:, units],
            g_s.at[k], g_r.at[k], (upward, downward)[way],
        )

    def half_of(k, half):
        return gd_in.at[k, pl.ds(half * HALF, HALF)]

    def send_two(part):
        send_gd((2, 0), part, 0, gd_half.at[0])
        send_gd((2, 1), part, 1, gd_half.at[1])

    def send_one(part):
        send_gd((1, 1), part, 0, half_of(0, 1))
        send_gd((3, 0), part, 1, half_of(1, 0))

    def send_rest(part):
        gd[(2, 0), part].wait_recv()
        send_gd((1, 0), part, 0, half_of(0, 0), gd_half.at[0])
        gd[(2, 1), part].wait_recv()
        send_gd((3, 1), part, 1, half_of(1, 1), gd_half.at[1])

    for j in range(4):
        arrive(0, 0, j)
        ring_chunk(1, 0, j)
        if j == 2:
            w_up.wait_recv()
            w_rest.append(send_w(4, (3, 0), (2, 0), upward))
            w_down.wait_recv()
            w_rest.append(send_w(5, (1, 1), (2, 1), downward))
    pass_h(0)
    for j in range(4):
        arrive(1, 0, j)
        ring_chunk(2, 0, j)
    ring_chunk(1, 1)
    arrive_h(0)
    early_down(0)
    pass_h(1)
    for j in range(4):
        arrive(2, 0, j)
        ring_chunk(3, 0, j)
    for copy in w_rest:
        copy.wait_recv()
    partial_hidden(0)
    arrive(1, 1)
    ring_chunk(2, 1)
    ring_chunk(1, 2)
    pass_h(2)
    add_peer(0)
    send_far(0)
    arrive_h(1)
    for j in range(4):
        arrive(3, 0, j)
    late_down(0, 0)
    send_two(0)
    partial_hidden(1, 0, CHUNKS[2][0])
    arrive(2, 1)
    ring_chunk(1, 3)
    ring_chunk(3, 1)
    arrive_h(2)
    early_down(1)
    pass_h(3)
    arrive(1, 2)
    ring_chunk(2, 2)
    partial_hidden(1, *CHUNKS[2])
    arrive_h(3)
    late_down(0, 1)
    send_two(1)
    arrive(1, 3)
    ring_chunk(2, 3)
    partial_hidden(1, *CHUNKS[3])
    add_peer(1)
    send_far(1)
    arrive(3, 1)
    late_down(1, 0)
    send_one(0)
    late_down(1, 1)
    send_one(1)
    partial_hidden(2, 0, CHUNKS[2][0])
    arrive(2, 2)
    ring_chunk(3, 2)
    partial_hidden(2, *CHUNKS[2])
    partial_hidden(3, 0, CHUNKS[2][0])
    arrive(2, 3)
    ring_chunk(3, 3)
    partial_hidden(2, *CHUNKS[3])
    add_peer(2)
    send_far(2)
    arrive(3, 2)
    late_down(2, 0)
    send_rest(0)
    late_down(2, 1)
    send_rest(1)
    arrive(3, 3)
    partial_hidden(3, CHUNKS[2][0], QD - CHUNKS[2][0])
    late_down(3, 0)
    add_peer(3)
    send_far(3)
    late_down(3, 1)
    for i in range(3):
        finish_hidden(i)
    for part in range(2):
        for unit in ((1, 0), (1, 1), (3, 0), (3, 1)):
            gd[unit, part].wait_recv()
    grad_down[...] = (
        acc[pl.ds(POS[0, 0], OWN), :] + gd_in[0].astype(F32) + gd_in[1].astype(F32)
    ).astype(BF16)
    finish_hidden(3)
    for copy in started:
        copy.wait_send()


def write_out(*refs):
    copies = [
        pltpu.make_async_copy(refs[i], refs[3 + i], refs[6].at[i]) for i in range(3)
    ]
    for copy in copies:
        copy.start()
    for copy in copies:
        copy.wait()


def on_device(gate_pre, up_saved, cotangent, down_weight):
    vmem = pl.BlockSpec(memory_space=pltpu.VMEM)
    dma = pltpu.SemaphoreType.DMA
    tokens = (2, 8, ROWS, FF)
    shapes = (tokens, tokens, (OWN, FF))
    results = pl.pallas_call(
        kernel,
        name="ffn_down_backward",
        out_shape=tuple(pltpu.VMEM(shape, BF16) for shape in shapes),
        in_specs=[pl.BlockSpec(memory_space=pl.ANY)] * 4,
        out_specs=(vmem,) * 3,
        scratch_shapes=[
            pltpu.VMEM(tokens, BF16),
            pltpu.VMEM(tokens, BF16),
            pltpu.VMEM((ROWS, D), BF16),
            pltpu.VMEM((4, ROWS, QD), BF16),
            pltpu.VMEM((8, 2, 4, ROWS, QD), BF16),
            pltpu.VMEM((QD, FF), BF16),
            pltpu.VMEM((8, 2, 4, ROWS, FF), BF16),
            pltpu.VMEM((8, 2, ROWS, FF), F32),
            pltpu.VMEM((8, 2, ROWS, FF), F32),
            pltpu.VMEM((QD, FF), F32),
            pltpu.VMEM((8, 4, ROWS, FF), BF16),
            pltpu.VMEM((8, 4, ROWS, FF), BF16),
            pltpu.VMEM((8, 4, ROWS, FF), F32),
            pltpu.VMEM((LATE[1], 4, ROWS, FF), F32),
            pltpu.VMEM((8, 2, ROWS, FF), BF16),
            pltpu.VMEM((8, 2, ROWS, FF), BF16),
            pltpu.VMEM((QD, FF), BF16),
            pltpu.VMEM((2, HALF, FF), BF16),
            pltpu.VMEM((2, OWN, FF), BF16),
            dma((4,)), dma((7,)), dma((7,)),
            dma((2, 25)), dma((2, 25)),
            dma((6,)), dma((6,)),
            dma((3, 4)), dma((3, 4)),
            dma((4,)), dma((4,)),
            dma((4,)), dma((4,)),
            dma((12,)), dma((12,)),
        ],
        compiler_params=pltpu.CompilerParams(
            collective_id=0, has_side_effects=True, vmem_limit_bytes=52 << 20
        ),
        cost_estimate=pl.CostEstimate(
            flops=4 * 2048 * QD * FF, bytes_accessed=7 << 20, transcendentals=512 * FF
        ),
    )(
        gate_pre.reshape(tokens), up_saved.reshape(tokens), cotangent, down_weight
    )
    grad_gate, grad_up, grad_down = pl.pallas_call(
        write_out,
        name="write_out",
        out_shape=tuple(jax.ShapeDtypeStruct(shape, BF16) for shape in shapes),
        in_specs=[vmem] * 3,
        out_specs=(pl.BlockSpec(memory_space=pl.ANY),) * 3,
        scratch_shapes=[dma((3,))],
        compiler_params=pltpu.CompilerParams(vmem_limit_bytes=8 << 20),
    )(*[pltpu.with_memory_space_constraint(r, pltpu.VMEM) for r in results])
    return (grad_gate.reshape(512, FF), grad_up.reshape(512, FF), grad_down)


def solution(mesh):
    in_specs = (P("dp", "tensor"), P("dp", "tensor"), P(("dp", "tensor"), None), P("dp", "tensor"))
    out_specs = (P("dp", "tensor"), P("dp", "tensor"), P("dp", "tensor"))
    return jax.shard_map(
        on_device, mesh=mesh, in_specs=in_specs, out_specs=out_specs, check_vma=False
    )
```
